256 devices in a mesh: replica: 4 (over y), fsdp: 64 (over z, x, core).
Axes of the slice: x: 4, y: 4, z: 8, core: 2. Of those that a mesh axis runs over, the one named last changes fastest.
Arguments:
- grads: bfloat16 [4, 64, 1024, 1024], P('replica', None, 'fsdp')
- block_owner: int32 [64], replicated, may hold values from 0 to 63, as said below
- left_roots: bfloat16 [128, 1024, 1024], P('fsdp')
- right_roots: bfloat16 [128, 1024, 1024], P('fsdp')
Outputs:
- direction: bfloat16 [64, 1024, 1024], P(None, 'fsdp')
The draws below stay inside these ranges and needn't reach their ends.
Inputs may be any that keep to these rules, and one draw needn't show every extreme that they name: `block_owner`: each fsdp rank owns at most 2 blocks, and some rank owns exactly 2.
All inputs are finite; a program needn't handle non-finite values.
Results may differ from the reference program's by a relative error of at most 0.017.
Values may be sent and summed in bfloat16 or wider, within the bound.
A program may use at most 128 MiB of HBM per device.

```python
import jax
import jax.numpy as jnp
from jax import lax

B = 1024
BLOCKS = 64
SLOTS = 2
N_REPLICA = 4
N_FSDP = 64


def draw_grads(key, part):
    key = jax.random.fold_in(key, 11)
    key_rows = jax.random.fold_in(key, 0)
    key_cols = jax.random.fold_in(key, 1)
    key_own = jax.random.fold_in(key, 3)
    row_scale = jnp.exp(jax.random.uniform(key_rows, (1, BLOCKS, B, 1), jnp.float32) * jnp.log(10.0))
    col_scale = jnp.exp(jax.random.uniform(key_cols, (1, BLOCKS, 1, B), jnp.float32) * jnp.log(10.0))
    steps_up = jnp.arange(N_REPLICA, dtype=jnp.float32) / max(N_REPLICA - 1, 1)
    rising = (1.0 + 2.0 * steps_up).reshape(N_REPLICA, 1, 1, 1)
    values = jax.random.normal(key_own, (N_REPLICA, BLOCKS, B, B), jnp.float32)
    return (0.05 * values * row_scale * col_scale * rising).astype(jnp.bfloat16)


def draw_block_owner(key, part):
    key = jax.random.fold_in(key, 5)
    key_ranks, key_picks, key_order = jax.random.split(key, 3)
    ranks = jax.random.permutation(key_ranks, N_FSDP).astype(jnp.int32)
    picks = jax.random.permutation(key_picks, (N_FSDP - 1) * SLOTS)[:BLOCKS - SLOTS].astype(jnp.int32)
    first_owner = jnp.full((SLOTS,), ranks[0], jnp.int32)
    others = ranks[1 + picks // SLOTS]
    owners = jnp.concatenate([first_owner, others]).astype(jnp.int32)
    order = jax.random.permutation(key_order, BLOCKS).astype(jnp.int32)
    return owners[order].astype(jnp.int32)


def root_matrix(diagonal, spread_part):
    positions = jnp.arange(B, dtype=jnp.int32)
    identity = (positions[:, None] == positions[None, :]).astype(jnp.float32)
    return identity[None, :, :] * diagonal[:, :, None] + spread_part


def draw_left_roots(key, part):
    key = jax.random.fold_in(key, 21)
    key_diag, key_off = jax.random.split(key, 2)
    diagonal = jax.random.uniform(key_diag, (N_FSDP * SLOTS, B), jnp.float32, 0.5, 2.0)
    spread_part = 0.02 * jax.random.normal(key_off, (N_FSDP * SLOTS, B, B), jnp.float32)
    return root_matrix(diagonal, spread_part).astype(jnp.bfloat16)


def draw_right_roots(key, part):
    key = jax.random.fold_in(key, 33)
    key_diag, key_off = jax.random.split(key, 2)
    diagonal = jax.random.uniform(key_diag, (N_FSDP * SLOTS, B), jnp.float32, 0.5, 2.0)
    spread_part = 0.02 * jax.random.normal(key_off, (N_FSDP * SLOTS, B, B), jnp.float32)
    return root_matrix(diagonal, spread_part).astype(jnp.bfloat16)


def setup_inputs(seed: int = 0) -> dict:
    key_of = jax.random.split(jax.random.key(seed), 5)
    grads = draw_grads(jax.random.fold_in(key_of[4], 71), 0)
    block_owner = draw_block_owner(jax.random.fold_in(key_of[4], 71), 0)
    left_roots = draw_left_roots(jax.random.fold_in(key_of[4], 71), 0)
    right_roots = draw_right_roots(jax.random.fold_in(key_of[4], 71), 0)
    return {"grads": grads, "block_owner": block_owner, "left_roots": left_roots, "right_roots": right_roots}


EPSILON = 1e-06

def slot_ranks(block_owner):
    same_owner = block_owner[:, None] == block_owner[None, :]
    positions = jnp.arange(block_owner.shape[0], dtype=jnp.int32)
    earlier = positions[None, :] < positions[:, None]
    return lax.optimization_barrier(jnp.sum(jnp.logical_and(same_owner, earlier).astype(jnp.int32), axis=1)).astype(jnp.int32)

def reference(grads, block_owner, left_roots, right_roots):
    summed = lax.optimization_barrier(jnp.sum(grads.astype(jnp.float32), axis=0)).astype(jnp.bfloat16)
    slot_keys = (block_owner * SLOTS + slot_ranks(block_owner)).astype(jnp.int32)

    def precondition(operands):
        block_grad, slot_key = operands
        left_root = lax.dynamic_index_in_dim(left_roots, slot_key, 0, keepdims=False)
        right_root = lax.dynamic_index_in_dim(right_roots, slot_key, 0, keepdims=False)
        middle = jnp.dot(left_root, block_grad, preferred_element_type=jnp.float32).astype(jnp.bfloat16)
        precond = jnp.dot(middle, right_root, preferred_element_type=jnp.float32)
        grad_ms = jnp.mean(jnp.square(block_grad.astype(jnp.float32)))
        pre_ms = jnp.mean(jnp.square(precond))
        factor = jnp.sqrt(grad_ms) * lax.rsqrt(pre_ms + EPSILON)
        return (precond * factor).astype(jnp.bfloat16)
    return lax.map(precondition, (summed, slot_keys))
```

```python
import jax
import jax.numpy as jnp
from jax import lax
from jax.experimental import pallas as pl
from jax.experimental.pallas import tpu as pltpu
from jax.sharding import PartitionSpec as P

EPSILON = 1e-06
MESH = pl.DeviceIdType.MESH

NY, NZ, NX = 4, 8, 4
RANKS = 64
CHIPS = NY * NZ * NX
BLOCKS = 64
HALF = BLOCKS // 2
ROWS = 16
SIDE = 1024
COLS = SIDE // NY
TILE = 256


def rem(a, b):
    return lax.rem(a, jnp.int32(b))


def div(a, b):
    return lax.div(a, jnp.int32(b))


def columns(quarter):
    return pl.ds(pl.multiple_of(quarter * COLS, COLS), COLS)


def offset(i, r, z, x):
    m, j = rem(i, NZ), div(i, NZ)
    dz = rem(3 * m, NZ)
    dx = rem(j + m, NX)
    dy = rem(div(j, NX) + m, NY)
    return rem(r + dy, NY), rem(z + dz, NZ), rem(x + dx, NX)


def kernel(holder, home, g_hbm, l_hbm, r_hbm, o, g, ta, tb, ca, cb, ra, rb, outgoing, s_ref, l_ref, r_ref, pf, d_ref,
           back, load_sem, rs_send, rs_recv, f_send, f_recv, b_send, b_recv, ag_send, ag_recv, sem_z, sem_x):
    r, f = lax.axis_index("replica"), lax.axis_index("fsdp")
    z, x, c = div(f, 8), rem(div(f, 2), NX), rem(f, 2)
    in_plane = rem(f, 8)
    slot = div(r, 2)
    active = rem(r, 2) == c
    key = 2 * f + slot

    load_g = pltpu.make_async_copy(g_hbm.at[0], g, load_sem.at[0])
    load_l = pltpu.make_async_copy(l_hbm.at[slot], l_ref, load_sem.at[1])
    load_r = pltpu.make_async_copy(r_hbm.at[slot], r_ref, load_sem.at[2])
    load_g.start()
    load_l.start()
    load_r.start()

    def z_peer(d):
        return (r, rem(z + d, NZ) * 8 + in_plane)

    def x_peer(d):
        return (r, z * 8 + rem(in_plane + d, 8))

    barrier = pltpu.get_barrier_semaphore()
    for d in range(1, NY):
        pl.semaphore_signal(barrier, inc=1, device_id=(rem(r + d, NY), f), device_id_type=MESH)

    def greet(d, _):
        pl.semaphore_signal(barrier, inc=1, device_id=z_peer(d), device_id_type=MESH)
        pl.semaphore_signal(barrier, inc=1, device_id=x_peer(d), device_id_type=MESH)
        return 0

    lax.fori_loop(1, 8, greet, 0)
    pl.semaphore_wait(barrier, 17)

    up, dn, opp = rem(r + 1, NY), rem(r + 3, NY), rem(r + 2, NY)
    low, high = pl.ds(0, HALF), pl.ds(HALF, HALF)

    def remote(n, src, dst, send, recv, plane):
        return pltpu.make_async_remote_copy(
            src_ref=src, dst_ref=dst, send_sem=send.at[n], recv_sem=recv.at[n], device_id=(plane, f), device_id_type=MESH
        )

    load_g.wait()
    far_up = remote(0, g.at[low, :, columns(opp)], ta, rs_send, rs_recv, up)
    far_dn = remote(1, g.at[high, :, columns(opp)], tb, rs_send, rs_recv, dn)
    near_up = remote(2, g.at[high, :, columns(up)], ra.at[high], rs_send, rs_recv, up)
    near_dn = remote(3, g.at[low, :, columns(dn)], rb.at[low], rs_send, rs_recv, dn)
    sum_up = remote(4, ca, ra.at[low], rs_send, rs_recv, up)
    sum_dn = remote(5, cb, rb.at[high], rs_send, rs_recv, dn)
    far_up.start()
    far_dn.start()
    near_up.start()
    near_dn.start()

    def greet_z(d, _):
        pl.semaphore_signal(sem_z, inc=1, device_id=z_peer(d), device_id_type=MESH)
        return 0

    def greet_x(d, _):
        pl.semaphore_signal(sem_x, inc=1, device_id=x_peer(d), device_id_type=MESH)
        return 0

    lax.fori_loop(1, 8, greet_z, 0)
    pl.semaphore_wait(sem_z, 7)
    lax.fori_loop(1, 8, greet_x, 0)
    pl.semaphore_wait(sem_x, 7)

    def add_up(b, _):
        ca[b] = (g[b, :, columns(up)].astype(jnp.float32) + ta[b].astype(jnp.float32)).astype(jnp.bfloat16)
        return 0

    def add_dn(b, _):
        mine = g[b + HALF, :, columns(dn)].astype(jnp.float32)
        cb[b] = (mine + tb[b].astype(jnp.float32)).astype(jnp.bfloat16)
        return 0

    far_up.wait_recv()
    lax.fori_loop(0, HALF, add_up, 0)
    sum_up.start()
    far_dn.wait_recv()
    lax.fori_loop(0, HALF, add_dn, 0)
    sum_dn.start()
    for copy in (near_up, near_dn, sum_up, sum_dn):
        copy.wait_recv()
    for copy in (far_up, far_dn, near_up, near_dn, sum_up, sum_dn):
        copy.wait_send()

    mine = columns(r)
    my_rows = pl.ds(pl.multiple_of(f * ROWS, ROWS), ROWS)

    def pack(i, rank, slot_of):
        h = holder[2 * rank + slot_of]
        total = g[h, :, mine].astype(jnp.float32) + ra[h].astype(jnp.float32) + rb[h].astype(jnp.float32)
        outgoing[i] = total.astype(jnp.bfloat16)

    def send_rows(i, plane, rank):
        return pltpu.make_async_remote_copy(
            src_ref=outgoing.at[i], dst_ref=s_ref.at[my_rows, mine], send_sem=f_send, recv_sem=f_recv,
            device_id=(plane, rank), device_id_type=MESH,
        )

    def forward(i, _):
        plane, tz, tx = offset(i, r, z, x)
        rank = tz * 8 + tx * 2 + rem(plane, 2)
        pack(i, rank, div(plane, 2))
        send_rows(i, plane, rank).start()
        return 0

    lax.fori_loop(1, CHIPS, forward, 0)
    home_rank = f - c + rem(r, 2)
    pack(0, home_rank, slot)

    @pl.when(active)
    def _():
        pltpu.make_async_copy(outgoing.at[0], s_ref.at[my_rows, mine], f_recv).start()

    @pl.when(jnp.logical_not(active))
    def _():
        send_rows(0, r, home_rank).start()
        pltpu.make_async_copy(outgoing.at[0], outgoing.at[0], f_send).wait()

    rest = outgoing.at[pl.ds(1, CHIPS - 1)]
    pltpu.make_async_copy(rest, rest, f_send).wait()

    def send_back(i, plane, rank, core):
        to = rank + core
        rows = pl.ds(pl.multiple_of(to * ROWS, ROWS), ROWS)
        return pltpu.make_async_remote_copy(
            src_ref=d_ref.at[rows, columns(plane)], dst_ref=back.at[key], send_sem=b_send, recv_sem=b_recv,
            device_id=(plane, to), device_id_type=MESH,
        )

    load_l.wait()
    load_r.wait()

    @pl.when(active)
    def _():
        pltpu.make_async_copy(s_ref, s_ref, f_recv).wait()

        def product(t, carry):
            grad_sq, pre_sq = carry
            rows = pl.ds(pl.multiple_of(t * TILE, TILE), TILE)
            middle = jnp.dot(l_ref[rows, :], s_ref[...], preferred_element_type=jnp.float32).astype(jnp.bfloat16)
            pre = jnp.dot(middle, r_ref[...], preferred_element_type=jnp.float32)
            pf[rows, :] = pre
            grad_sq = grad_sq + jnp.sum(jnp.square(s_ref[rows, :].astype(jnp.float32)), axis=0, keepdims=True)
            pre_sq = pre_sq + jnp.sum(jnp.square(pre), axis=0, keepdims=True)
            return grad_sq, pre_sq

        zero = jnp.zeros((1, SIDE), jnp.float32)
        grad_sq, pre_sq = lax.fori_loop(0, SIDE // TILE, product, (zero, zero))
        grad_ms = jnp.sum(grad_sq, axis=1, keepdims=True) / (SIDE * SIDE)
        pre_ms = jnp.sum(pre_sq, axis=1, keepdims=True) / (SIDE * SIDE)
        factor = jnp.sqrt(grad_ms) * lax.rsqrt(pre_ms + EPSILON)

        def scale(t, _):
            rows = pl.ds(pl.multiple_of(t * TILE, TILE), TILE)
            d_ref[rows, :] = (pf[rows, :] * factor).astype(jnp.bfloat16)
            return 0

        lax.fori_loop(0, SIDE // TILE, scale, 0)

        def backward(i, _):
            plane, tz, tx = offset(i, r, z, x)
            rank = tz * 8 + tx * 2
            send_back(i, plane, rank, 0).start()
            send_back(i, plane, rank, 1).start()
            return 0

        lax.fori_loop(1, CHIPS, backward, 0)
        send_back(0, r, f - c, 1 - c).start()
        pltpu.make_async_copy(d_ref.at[my_rows, mine], back.at[key], b_recv).start()
        sent = d_ref.at[pl.ds(0, SIDE - ROWS), :]
        pltpu.make_async_copy(sent, sent, b_send).wait()
        last = d_ref.at[pl.ds(0, ROWS), pl.ds(0, SIDE - COLS)]
        pltpu.make_async_copy(last, last, b_send).wait()

    pltpu.make_async_copy(back, back, b_recv).wait()

    def place(b, _):
        o[b, :, mine] = back[home[b]]
        return 0

    def spread(n, half, quarter, plane):
        part = o.at[half, :, columns(quarter)]
        return remote(n, part, part, ag_send, ag_recv, plane)

    lax.fori_loop(0, HALF, place, 0)
    low_up, low_dn = spread(0, low, r, up), spread(1, low, r, dn)
    high_up, high_dn = spread(2, high, r, up), spread(3, high, r, dn)
    low_up.start()
    lax.fori_loop(HALF, BLOCKS, place, 0)
    high_dn.start()
    high_up.start()
    low_dn.start()
    on_up, on_dn = spread(4, low, dn, up), spread(5, high, up, dn)
    low_up.wait_recv()
    on_up.start()
    high_dn.wait_recv()
    on_dn.start()
    for copy in (high_up, low_dn, on_up, on_dn):
        copy.wait_recv()
    for copy in (low_up, high_dn, high_up, low_dn, on_up, on_dn):
        copy.wait_send()


def on_device(grads, block_owner, left_roots, right_roots):
    same_owner = block_owner[:, None] == block_owner[None, :]
    positions = jnp.arange(BLOCKS, dtype=jnp.int32)
    earlier = positions[None, :] < positions[:, None]
    slot_rank = jnp.sum(jnp.logical_and(same_owner, earlier).astype(jnp.int32), axis=1)
    home = 2 * block_owner + slot_rank
    matches = home[:, None] == jnp.arange(2 * RANKS, dtype=jnp.int32)[None, :]
    holder = jnp.sum(jnp.where(matches, positions[:, None], 0), axis=0)
    bf16, f32 = jnp.bfloat16, jnp.float32
    smem, anywhere = pl.BlockSpec(memory_space=pltpu.SMEM), pl.BlockSpec(memory_space=pl.ANY)
    return pl.pallas_call(
        kernel,
        out_shape=jax.ShapeDtypeStruct((BLOCKS, ROWS, SIDE), bf16),
        in_specs=[smem, smem, anywhere, anywhere, anywhere],
        out_specs=pl.BlockSpec(memory_space=pltpu.VMEM),
        scratch_shapes=[
            pltpu.VMEM((BLOCKS, ROWS, SIDE), bf16),
            pltpu.VMEM((HALF, ROWS, COLS), bf16),
            pltpu.VMEM((HALF, ROWS, COLS), bf16),
            pltpu.VMEM((HALF, ROWS, COLS), bf16),
            pltpu.VMEM((HALF, ROWS, COLS), bf16),
            pltpu.VMEM((BLOCKS, ROWS, COLS), bf16),
            pltpu.VMEM((BLOCKS, ROWS, COLS), bf16),
            pltpu.VMEM((CHIPS, ROWS, COLS), bf16),
            pltpu.VMEM((SIDE, SIDE), bf16),
            pltpu.VMEM((SIDE, SIDE), bf16),
            pltpu.VMEM((SIDE, SIDE), bf16),
            pltpu.VMEM((SIDE, SIDE), f32),
            pltpu.VMEM((SIDE, SIDE), bf16),
            pltpu.VMEM((CHIPS, ROWS, COLS), bf16),
            pltpu.SemaphoreType.DMA((3,)),
            pltpu.SemaphoreType.DMA((6,)),
            pltpu.SemaphoreType.DMA((6,)),
            pltpu.SemaphoreType.DMA,
            pltpu.SemaphoreType.DMA,
            pltpu.SemaphoreType.DMA,
            pltpu.SemaphoreType.DMA,
            pltpu.SemaphoreType.DMA((6,)),
            pltpu.SemaphoreType.DMA((6,)),
            pltpu.SemaphoreType.REGULAR,
            pltpu.SemaphoreType.REGULAR,
        ],
        compiler_params=pltpu.CompilerParams(
            collective_id=0, has_side_effects=True, vmem_limit_bytes=40 * 1024 * 1024
        ),
        cost_estimate=pl.CostEstimate(flops=4 * SIDE**3, bytes_accessed=8 * 1024 * 1024, transcendentals=0),
    )(holder, home, grads, left_roots, right_roots)


def solution(mesh):
    in_specs = (P("replica", None, "fsdp", None), P(), P("fsdp", None, None), P("fsdp", None, None))
    return jax.shard_map(
        on_device, mesh=mesh, in_specs=in_specs, out_specs=P(None, "fsdp", None), check_vma=False
    )
```

```python
import jax
import jax.numpy as jnp
from jax import lax
from jax.experimental import pallas as pl
from jax.experimental.pallas import tpu as pltpu
from jax.sharding import PartitionSpec as P

EPSILON = 1e-06
MESH = pl.DeviceIdType.MESH

NY, NZ, NX = 4, 8, 4
COLUMNS = NZ * NX
BLOCKS = 64
SHARE = BLOCKS // NY
HALF = SHARE // 2
ROWS = 16
SIDE = 1024
CHUNKS = 4
WIDTH = SIDE // CHUNKS
TILE = 512

BLOCK_OF, ENTRY_OF, CELL, PAIR, COLUMN_OF = range(5)


def rem(a, b):
    return lax.rem(a, jnp.int32(b))


def div(a, b):
    return lax.div(a, jnp.int32(b))


def chunk(k):
    return pl.ds(k * WIDTH, WIDTH)


def f32(a):
    return a.astype(jnp.float32)


def bf16(a):
    return a.astype(jnp.bfloat16)


def make_table(owner, owners, table):
    lane1 = lax.broadcasted_iota(jnp.int32, (1, 128), 1)

    def spread(b, row):
        value = owner[b]
        owners[pl.ds(b, 1), :] = jnp.full((1, 128), value, jnp.int32)
        return jnp.where(lane1 == b, value, row)

    across = lax.fori_loop(0, BLOCKS, spread, jnp.full((1, 128), 4096, jnp.int32))
    down = owners[...]
    lane = lax.broadcasted_iota(jnp.int32, (BLOCKS, 128), 1)
    sub = lax.broadcasted_iota(jnp.int32, (BLOCKS, 128), 0)
    one, zero = jnp.ones((BLOCKS, 128), jnp.int32), jnp.zeros((BLOCKS, 128), jnp.int32)
    same = down == across
    earlier = jnp.logical_and(same, lane < sub)
    place = jnp.sum(jnp.where(jnp.logical_or(across < down, earlier), one, zero), axis=1, keepdims=True)
    slot = jnp.sum(jnp.where(earlier, one, zero), axis=1, keepdims=True)
    later = jnp.logical_or(down < across, jnp.logical_and(same, sub < lane))
    place_across = jnp.sum(jnp.where(later, one, zero), axis=0, keepdims=True)
    plane, position = place & 3, place >> 2
    column = down >> 1
    entry = jnp.where(plane * SHARE + position == lane, one, zero)
    here = jnp.where(jnp.logical_and(plane == (lane >> 5), column == (lane & 31)), one, zero)
    block = jnp.sum(entry * sub, axis=0, keepdims=True)
    cell = jnp.sum(here * position, axis=0, keepdims=True)
    pair = jnp.sum(here * (2 * (down & 1) + slot), axis=0, keepdims=True)
    column_of = jnp.sum(entry * column, axis=0, keepdims=True)
    table[pl.ds(BLOCK_OF, 1), :] = block & (BLOCKS - 1)
    table[pl.ds(ENTRY_OF, 1), :] = ((place_across & 3) * SHARE + (place_across >> 2)) & (BLOCKS - 1)
    table[pl.ds(CELL, 1), :] = cell & (SHARE - 1)
    table[pl.ds(PAIR, 1), :] = pair & 3
    table[pl.ds(COLUMN_OF, 1), :] = column_of & (COLUMNS - 1)


def kernel(owner, g_hbm, l_hbm, r_hbm, o, owners, table_v, table, g, gs, ta, tb, ca, cb, ra, rb, summed, outgoing, s_ref,
           l_ref, r_ref, pf, factor_ref, d_ref, load_sem, pair_send, pair_recv, rs_send, rs_recv, f_send, f_recv, b_send,
           b_recv, ag_send, ag_recv, plane_sem, *by_chunk):
    back, fin = by_chunk[:CHUNKS], by_chunk[CHUNKS:]
    r, f = lax.axis_index("replica"), lax.axis_index("fsdp")
    z, x, c = div(f, 8), rem(div(f, 2), NX), rem(f, 2)
    in_line = rem(f, 8)
    column = div(f, 2)
    worker = rem(r, 2)
    active = worker == c
    idle = jnp.logical_not(active)
    sibling = f + 1 - 2 * c

    load_g = pltpu.make_async_copy(g_hbm.at[0], g, load_sem.at[0])
    load_g.start()

    def z_peer(d):
        return (r, rem(z + d, NZ) * 8 + in_line)

    barrier = pltpu.get_barrier_semaphore()
    for d in range(1, NY):
        pl.semaphore_signal(barrier, inc=1, device_id=(rem(r + d, NY), f), device_id_type=MESH)

    def greet(d, _):
        pl.semaphore_signal(barrier, inc=1, device_id=z_peer(d), device_id_type=MESH)
        pl.semaphore_signal(barrier, inc=1, device_id=(r, z * 8 + rem(in_line + d, 8)), device_id_type=MESH)
        return 0

    lax.fori_loop(1, 8, greet, 0)

    make_table(owner, owners, table_v)
    load_table = pltpu.make_async_copy(table_v, table, load_sem.at[1])
    load_table.start()

    pl.semaphore_wait(barrier, 17)

    def greet_plane(d, _):
        pl.semaphore_signal(plane_sem, inc=1, device_id=z_peer(d), device_id_type=MESH)
        return 0

    lax.fori_loop(1, 8, greet_plane, 0)

    own_pairs = pl.ds(2 * c, 2)
    load_l = pltpu.make_async_copy(l_hbm, l_ref.at[own_pairs], load_sem.at[2])
    load_r = pltpu.make_async_copy(r_hbm, r_ref.at[own_pairs], load_sem.at[3])

    def give(n, src, dst):
        return pltpu.make_async_remote_copy(
            src_ref=src, dst_ref=dst.at[own_pairs], send_sem=pair_send.at[n], recv_sem=pair_recv.at[n],
            device_id=(r, sibling), device_id_type=MESH,
        )

    give_l, give_r = give(0, l_hbm, l_ref), give(1, r_hbm, r_ref)

    up, dn, opp = rem(r + 1, NY), rem(r + 3, NY), rem(r + 2, NY)
    low, high = pl.ds(0, HALF), pl.ds(HALF, HALF)

    def half_of(plane, n):
        return pl.ds(plane * SHARE + n * HALF, HALF)

    def remote(n, src, dst, send, recv, plane):
        return pltpu.make_async_remote_copy(
            src_ref=src, dst_ref=dst, send_sem=send.at[n], recv_sem=recv.at[n], device_id=(plane, f), device_id_type=MESH
        )

    def sum_copies(k):
        ck, n = chunk(k), 6 * k
        return (
            remote(n, gs.at[half_of(opp, 0), :, ck], ta.at[:, :, ck], rs_send, rs_recv, up),
            remote(n + 1, gs.at[half_of(opp, 1), :, ck], tb.at[:, :, ck], rs_send, rs_recv, dn),
            remote(n + 2, gs.at[half_of(up, 1), :, ck], ra.at[high, :, ck], rs_send, rs_recv, up),
            remote(n + 3, gs.at[half_of(dn, 0), :, ck], rb.at[low, :, ck], rs_send, rs_recv, dn),
            remote(n + 4, ca.at[:, :, ck], ra.at[low, :, ck], rs_send, rs_recv, up),
            remote(n + 5, cb.at[:, :, ck], rb.at[high, :, ck], rs_send, rs_recv, dn),
        )

    sums = [sum_copies(k) for k in range(CHUNKS)]

    def sum_first(k):
        ck = chunk(k)

        def pack(e, _):
            gs[e, :, ck] = g[table[BLOCK_OF, e], :, ck]
            return 0

        lax.fori_loop(0, BLOCKS, pack, 0, unroll=4)
        for copy in sums[k][:4]:
            copy.start()

    def sum_second(k):
        ck = chunk(k)

        def add_up(i, _):
            ca[i, :, ck] = bf16(f32(gs[up * SHARE + i, :, ck]) + f32(ta[i, :, ck]))
            return 0

        def add_dn(i, _):
            cb[i, :, ck] = bf16(f32(gs[dn * SHARE + HALF + i, :, ck]) + f32(tb[i, :, ck]))
            return 0

        sums[k][0].wait_recv()
        lax.fori_loop(0, HALF, add_up, 0, unroll=4)
        sums[k][4].start()
        sums[k][1].wait_recv()
        lax.fori_loop(0, HALF, add_dn, 0, unroll=4)
        sums[k][5].start()

    def offset(n):
        m = rem(n, NZ)
        dz, dx = rem(3 * m, NZ), rem(div(n, NZ) + m, NX)
        return rem(z + dz, NZ) * NX + rem(x + dx, NX)

    def rows_of(rank):
        return pl.ds(pl.multiple_of(rank * ROWS, ROWS), ROWS)

    def forward(k):
        ck = chunk(k)
        for copy in sums[k][2:]:
            copy.wait_recv()

        def add(i, _):
            total = f32(gs[r * SHARE + i, :, ck]) + f32(ra[i, :, ck]) + f32(rb[i, :, ck])
            summed[i, :, ck] = bf16(total)
            return 0

        lax.fori_loop(0, SHARE, add, 0, unroll=4)

        def pack(q):
            outgoing[q, :, ck] = summed[table[CELL, r * COLUMNS + q], :, ck]

        def send(q):
            return pltpu.make_async_remote_copy(
                src_ref=outgoing.at[q, :, ck], dst_ref=s_ref.at[rows_of(f), ck], send_sem=f_send, recv_sem=f_recv.at[k],
                device_id=(r, 2 * q + worker), device_id_type=MESH,
            )

        def step(n, _):
            q = offset(n)
            pack(q)
            send(q).start()
            return 0

        lax.fori_loop(1, COLUMNS, step, 0)
        pack(column)

        @pl.when(active)
        def _():
            pltpu.make_async_copy(outgoing.at[column, :, ck], s_ref.at[rows_of(f), ck], f_recv.at[k]).start()

        @pl.when(idle)
        def _():
            send(column).start()

    def products(first, count):
        part = pl.ds(first * WIDTH, count * WIDTH)
        for k in range(first, first + count):
            pltpu.make_async_copy(s_ref.at[:, chunk(k)], s_ref.at[:, chunk(k)], f_recv.at[k]).wait()
        pair = table[PAIR, r * COLUMNS + column]
        last = first + count == CHUNKS

        def step(t, carry):
            grad_sq, pre_sq = carry
            rows = pl.ds(pl.multiple_of(t * TILE, TILE), TILE)
            middle = bf16(jnp.dot(l_ref[pair, rows, :], s_ref[:, part], preferred_element_type=jnp.float32))
            pre = jnp.dot(middle, r_ref[pair, part, :], preferred_element_type=jnp.float32)
            if first > 0:
                pre = pre + pf[rows, :]
            pf[rows, :] = pre
            grad_sq = grad_sq + jnp.sum(jnp.square(f32(s_ref[rows, part])), axis=0, keepdims=True)
            if last:
                pre_sq = pre_sq + jnp.sum(jnp.square(pre), axis=0, keepdims=True)
            return grad_sq, pre_sq

        zeros = (jnp.zeros((1, count * WIDTH), jnp.float32), jnp.zeros((1, SIDE), jnp.float32))
        grad_sq, pre_sq = lax.fori_loop(0, SIDE // TILE, step, zeros)
        return jnp.sum(grad_sq, axis=1, keepdims=True), jnp.sum(pre_sq, axis=1, keepdims=True)

    def backward(k):
        ck = chunk(k)

        def send(rank):
            return pltpu.make_async_remote_copy(
                src_ref=d_ref.at[rows_of(rank), ck], dst_ref=back[k].at[column], send_sem=b_send, recv_sem=b_recv.at[k],
                device_id=(r, rank), device_id_type=MESH,
            )

        @pl.when(active)
        def _():
            factor = factor_ref[...]

            def scale(t, _):
                rows = pl.ds(pl.multiple_of(t * 128, 128), 128)
                d_ref[rows, ck] = bf16(pf[rows, ck] * factor)
                return 0

            lax.fori_loop(0, SIDE // 128, scale, 0)

            def step(n, _):
                q = offset(n)
                send(2 * q).start()
                send(2 * q + 1).start()
                return 0

            lax.fori_loop(1, COLUMNS, step, 0)
            send(sibling).start()
            pltpu.make_async_copy(d_ref.at[rows_of(f), ck], back[k].at[column], b_recv.at[k]).start()

    def gather_copies(k):
        n = 6 * k

        def spread(m, plane, half, to):
            part = fin[k].at[half_of(plane, half)]
            return remote(n + m, part, part, ag_send, ag_recv, to)

        return (
            spread(0, r, 0, up), spread(1, r, 1, dn), spread(2, r, 1, up), spread(3, r, 0, dn), spread(4, dn, 0, up),
            spread(5, up, 1, dn),
        )

    gathers = [gather_copies(k) for k in range(CHUNKS)]

    def gather_first(k):
        pltpu.make_async_copy(back[k], back[k], b_recv.at[k]).wait()

        def place(i, _):
            e = r * SHARE + i
            fin[k][e] = back[k][table[COLUMN_OF, e]]
            return 0

        lax.fori_loop(0, SHARE, place, 0, unroll=4)
        for copy in gathers[k][:4]:
            copy.start()

    def gather_second(k):
        gathers[k][0].wait_recv()
        gathers[k][4].start()
        gathers[k][1].wait_recv()
        gathers[k][5].start()

    def finish(k):
        ck = chunk(k)
        for copy in gathers[k][2:]:
            copy.wait_recv()

        def place(b, _):
            o[b, :, ck] = fin[k][table[ENTRY_OF, b]]
            return 0

        lax.fori_loop(0, BLOCKS, place, 0, unroll=4)

    load_g.wait()
    load_table.wait()
    sum_first(0)

    @pl.when(active)
    def _():
        load_l.start()
        load_r.start()

    @pl.when(idle)
    def _():
        give_l.start()
        give_r.start()

    pl.semaphore_wait(plane_sem, 7)
    sum_second(0)
    sum_first(1)
    forward(0)
    sum_second(1)
    sum_first(2)
    forward(1)
    sum_second(2)
    sum_first(3)
    forward(2)
    sum_second(3)
    forward(3)

    @pl.when(active)
    def _():
        load_l.wait()
        load_r.wait()
        give_l.wait_recv()
        give_r.wait_recv()
        grad_a, _ = products(0, 2)
        grad_b, _ = products(2, 1)
        grad_c, pre_sq = products(3, 1)
        grad_ms = (grad_a + grad_b + grad_c) / (SIDE * SIDE)
        pre_ms = pre_sq / (SIDE * SIDE)
        factor_ref[...] = jnp.sqrt(grad_ms) * lax.rsqrt(pre_ms + EPSILON)

    backward(0)
    backward(1)
    gather_first(0)
    backward(2)
    gather_first(1)
    gather_second(0)
    backward(3)
    gather_first(2)
    gather_second(1)
    finish(0)
    gather_first(3)
    gather_second(2)
    finish(1)
    gather_second(3)
    finish(2)
    finish(3)

    for copies in sums + gathers:
        for copy in copies:
            copy.wait_send()

    @pl.when(active)
    def _():
        sent = outgoing.at[pl.ds(1, COLUMNS - 1)]
        pltpu.make_async_copy(sent, sent, f_send).wait()
        sent = d_ref.at[pl.ds(0, SIDE - ROWS), :]
        pltpu.make_async_copy(sent, sent, b_send).wait()

    @pl.when(idle)
    def _():
        pltpu.make_async_copy(outgoing, outgoing, f_send).wait()
        give_l.wait_send()
        give_r.wait_send()


def on_device(grads, block_owner, left_roots, right_roots):
    anywhere = pl.BlockSpec(memory_space=pltpu.HBM)
    share = pltpu.VMEM((SHARE, ROWS, SIDE), jnp.bfloat16)
    half = pltpu.VMEM((HALF, ROWS, SIDE), jnp.bfloat16)
    column = pltpu.VMEM((COLUMNS, ROWS, SIDE), jnp.bfloat16)
    whole = pltpu.VMEM((BLOCKS, ROWS, SIDE), jnp.bfloat16)
    square = pltpu.VMEM((SIDE, SIDE), jnp.bfloat16)
    roots = pltpu.VMEM((4, SIDE, SIDE), jnp.bfloat16)
    dma = pltpu.SemaphoreType.DMA
    return pl.pallas_call(
        kernel,
        out_shape=jax.ShapeDtypeStruct((BLOCKS, ROWS, SIDE), jnp.bfloat16),
        in_specs=[pl.BlockSpec(memory_space=pltpu.SMEM), anywhere, anywhere, anywhere],
        out_specs=pl.BlockSpec(memory_space=pltpu.VMEM),
        scratch_shapes=[
            pltpu.VMEM((BLOCKS, 128), jnp.int32), pltpu.VMEM((8, 128), jnp.int32), pltpu.SMEM((8, 128), jnp.int32),
            whole, whole, half, half, half, half, share, share, share, column, square, roots, roots,
            pltpu.VMEM((SIDE, SIDE), jnp.float32), pltpu.VMEM((1, 1), jnp.float32), square,
            dma((4,)), dma((2,)), dma((2,)), dma((6 * CHUNKS,)), dma((6 * CHUNKS,)), dma, dma((CHUNKS,)), dma, dma((CHUNKS,)),
            dma((6 * CHUNKS,)), dma((6 * CHUNKS,)), pltpu.SemaphoreType.REGULAR,
            *[pltpu.VMEM((COLUMNS, ROWS, WIDTH), jnp.bfloat16)] * CHUNKS,
            *[pltpu.VMEM((BLOCKS, ROWS, WIDTH), jnp.bfloat16)] * CHUNKS,
        ],
        compiler_params=pltpu.CompilerParams(
            collective_id=0, has_side_effects=True, vmem_limit_bytes=48 * 1024 * 1024
        ),
        cost_estimate=pl.CostEstimate(flops=4 * SIDE**3, bytes_accessed=12 * 1024 * 1024, transcendentals=0),
    )(block_owner, grads, left_roots, right_roots)


def solution(mesh):
    in_specs = (P("replica", None, "fsdp", None), P(), P("fsdp", None, None), P("fsdp", None, None))
    return jax.shard_map(
        on_device, mesh=mesh, in_specs=in_specs, out_specs=P(None, "fsdp", None), check_vma=False
    )
```

```python
import jax
import jax.numpy as jnp
from jax import lax
from jax.experimental import pallas as pl
from jax.experimental.pallas import tpu as pltpu
from jax.sharding import PartitionSpec as P

EPSILON = 1e-06
MESH = pl.DeviceIdType.MESH

NY, NZ, NX = 4, 8, 4
COLUMNS = NZ * NX
BLOCKS = 64
SHARE = BLOCKS // NY
HALF = SHARE // 2
ROWS = 16
SIDE = 1024
OUT = (256, 256, 256, 256)
BACK = (256, 256, 256, 256)
PARTS = ((0, 2), (2, 1), (3, 1))
TILE = 512

BLOCK_OF, ENTRY_OF, CELL, PAIR, COLUMN_OF = range(5)


def rem(a, b):
    return lax.rem(a, jnp.int32(b))


def div(a, b):
    return lax.div(a, jnp.int32(b))


def chunk(widths, k, count=1):
    return pl.ds(sum(widths[:k]), sum(widths[k : k + count]))


def f32(a):
    return a.astype(jnp.float32)


def bf16(a):
    return a.astype(jnp.bfloat16)


def make_table(owner, owners, table):
    lane1 = lax.broadcasted_iota(jnp.int32, (1, 128), 1)

    def spread(b, row):
        value = owner[b]
        owners[pl.ds(b, 1), :] = jnp.full((1, 128), value, jnp.int32)
        return jnp.where(lane1 == b, value, row)

    across = lax.fori_loop(0, BLOCKS, spread, jnp.full((1, 128), 4096, jnp.int32))
    down = owners[...]
    lane = lax.broadcasted_iota(jnp.int32, (BLOCKS, 128), 1)
    sub = lax.broadcasted_iota(jnp.int32, (BLOCKS, 128), 0)
    one, zero = jnp.ones((BLOCKS, 128), jnp.int32), jnp.zeros((BLOCKS, 128), jnp.int32)
    same = down == across
    earlier = jnp.logical_and(same, lane < sub)
    place = jnp.sum(jnp.where(jnp.logical_or(across < down, earlier), one, zero), axis=1, keepdims=True)
    slot = jnp.sum(jnp.where(earlier, one, zero), axis=1, keepdims=True)
    later = jnp.logical_or(down < across, jnp.logical_and(same, sub < lane))
    place_across = jnp.sum(jnp.where(later, one, zero), axis=0, keepdims=True)
    plane, position = place & 3, place >> 2
    column = down >> 1
    entry = jnp.where(plane * SHARE + position == lane, one, zero)
    here = jnp.where(jnp.logical_and(plane == (lane >> 5), column == (lane & 31)), one, zero)
    block = jnp.sum(entry * sub, axis=0, keepdims=True)
    cell = jnp.sum(here * position, axis=0, keepdims=True)
    pair = jnp.sum(here * (2 * (down & 1) + slot), axis=0, keepdims=True)
    column_of = jnp.sum(entry * column, axis=0, keepdims=True)
    table[pl.ds(BLOCK_OF, 1), :] = block & (BLOCKS - 1)
    table[pl.ds(ENTRY_OF, 1), :] = ((place_across & 3) * SHARE + (place_across >> 2)) & (BLOCKS - 1)
    table[pl.ds(CELL, 1), :] = cell & (SHARE - 1)
    table[pl.ds(PAIR, 1), :] = pair & 3
    table[pl.ds(COLUMN_OF, 1), :] = column_of & (COLUMNS - 1)


def kernel(owner, g_hbm, l_hbm, r_hbm, o, owners, table_v, table, g, gs, ta, tb, ca, cb, ra, rb, summed, outgoing, s_ref,
           l_ref, r_ref, pf, factor_ref, d_ref, load_sem, pair_send, pair_recv, rs_send, rs_recv, f_send, f_recv, b_send,
           b_recv, d_send, d_recv, ag_send, ag_recv, plane_sem, *by_chunk):
    back, fin = by_chunk[: len(BACK)], by_chunk[len(BACK) :]
    r, f = lax.axis_index("replica"), lax.axis_index("fsdp")
    z, x, c = div(f, 8), rem(div(f, 2), NX), rem(f, 2)
    in_line = rem(f, 8)
    column = div(f, 2)
    worker = rem(r, 2)
    active = worker == c
    idle = jnp.logical_not(active)
    sibling = f + 1 - 2 * c

    load_g = pltpu.make_async_copy(g_hbm.at[0], g, load_sem.at[0])
    load_g.start()

    def z_peer(d):
        return (r, rem(z + d, NZ) * 8 + in_line)

    barrier = pltpu.get_barrier_semaphore()
    for d in range(1, NY):
        pl.semaphore_signal(barrier, inc=1, device_id=(rem(r + d, NY), f), device_id_type=MESH)

    def greet(d, _):
        pl.semaphore_signal(barrier, inc=1, device_id=z_peer(d), device_id_type=MESH)
        pl.semaphore_signal(barrier, inc=1, device_id=(r, z * 8 + rem(in_line + d, 8)), device_id_type=MESH)
        return 0

    lax.fori_loop(1, 8, greet, 0)

    make_table(owner, owners, table_v)
    load_table = pltpu.make_async_copy(table_v, table, load_sem.at[1])
    load_table.start()

    pl.semaphore_wait(barrier, 17)

    def greet_plane(d, _):
        pl.semaphore_signal(plane_sem, inc=1, device_id=z_peer(d), device_id_type=MESH)
        return 0

    lax.fori_loop(1, 8, greet_plane, 0)

    own_pairs = pl.ds(2 * c, 2)
    load_l = pltpu.make_async_copy(l_hbm, l_ref.at[own_pairs], load_sem.at[2])
    load_r = pltpu.make_async_copy(r_hbm, r_ref.at[own_pairs], load_sem.at[3])

    def give(n, src, dst):
        return pltpu.make_async_remote_copy(
            src_ref=src, dst_ref=dst.at[own_pairs], send_sem=pair_send.at[n], recv_sem=pair_recv.at[n],
            device_id=(r, sibling), device_id_type=MESH,
        )

    give_l, give_r = give(0, l_hbm, l_ref), give(1, r_hbm, r_ref)

    up, dn, opp = rem(r + 1, NY), rem(r + 3, NY), rem(r + 2, NY)
    low, high = pl.ds(0, HALF), pl.ds(HALF, HALF)

    def half_of(plane, n):
        return pl.ds(plane * SHARE + n * HALF, HALF)

    def remote(n, src, dst, send, recv, plane):
        return pltpu.make_async_remote_copy(
            src_ref=src, dst_ref=dst, send_sem=send.at[n], recv_sem=recv.at[n], device_id=(plane, f), device_id_type=MESH
        )

    def sum_copies(k):
        ck, n = chunk(OUT, k), 6 * k
        return (
            remote(n, gs.at[half_of(opp, 0), :, ck], ta.at[:, :, ck], rs_send, rs_recv, up),
            remote(n + 1, gs.at[half_of(opp, 1), :, ck], tb.at[:, :, ck], rs_send, rs_recv, dn),
            remote(n + 2, gs.at[half_of(up, 1), :, ck], ra.at[high, :, ck], rs_send, rs_recv, up),
            remote(n + 3, gs.at[half_of(dn, 0), :, ck], rb.at[low, :, ck], rs_send, rs_recv, dn),
            remote(n + 4, ca.at[:, :, ck], ra.at[low, :, ck], rs_send, rs_recv, up),
            remote(n + 5, cb.at[:, :, ck], rb.at[high, :, ck], rs_send, rs_recv, dn),
        )

    sums = [sum_copies(k) for k in range(len(OUT))]

    def sum_first(k):
        ck = chunk(OUT, k)

        def pack(e, _):
            gs[e, :, ck] = g[table[BLOCK_OF, e], :, ck]
            return 0

        lax.fori_loop(0, BLOCKS, pack, 0, unroll=4)
        for copy in sums[k][:4]:
            copy.start()

    def sum_second(k):
        ck = chunk(OUT, k)

        def add_up(i, _):
            ca[i, :, ck] = bf16(f32(gs[up * SHARE + i, :, ck]) + f32(ta[i, :, ck]))
            return 0

        def add_dn(i, _):
            cb[i, :, ck] = bf16(f32(gs[dn * SHARE + HALF + i, :, ck]) + f32(tb[i, :, ck]))
            return 0

        sums[k][0].wait_recv()
        lax.fori_loop(0, HALF, add_up, 0, unroll=4)
        sums[k][4].start()
        sums[k][1].wait_recv()
        lax.fori_loop(0, HALF, add_dn, 0, unroll=4)
        sums[k][5].start()

    def offset(n):
        def step(i, size):
            return rem(size // 2 + div(i + 1, 2) * (1 - 2 * rem(i, 2)), size)

        return rem(z + step(div(n, NX), NZ), NZ) * NX + rem(x + step(rem(n, NX), NX), NX)

    def rows_of(rank):
        return pl.ds(pl.multiple_of(rank * ROWS, ROWS), ROWS)

    def forward(k):
        ck = chunk(OUT, k)
        for copy in sums[k][2:]:
            copy.wait_recv()

        def add(i, _):
            total = f32(gs[r * SHARE + i, :, ck]) + f32(ra[i, :, ck]) + f32(rb[i, :, ck])
            summed[i, :, ck] = bf16(total)
            return 0

        lax.fori_loop(0, SHARE, add, 0, unroll=4)

        def pack(q):
            outgoing[q, :, ck] = summed[table[CELL, r * COLUMNS + q], :, ck]

        def send(q):
            return pltpu.make_async_remote_copy(
                src_ref=outgoing.at[q, :, ck], dst_ref=s_ref.at[rows_of(f), ck], send_sem=f_send, recv_sem=f_recv.at[k],
                device_id=(r, 2 * q + worker), device_id_type=MESH,
            )

        def step(n, _):
            q = offset(n)
            pack(q)
            send(q).start()
            return 0

        lax.fori_loop(0, COLUMNS - 1, step, 0)
        pack(column)

        @pl.when(active)
        def _():
            pltpu.make_async_copy(outgoing.at[column, :, ck], s_ref.at[rows_of(f), ck], f_recv.at[k]).start()

        @pl.when(idle)
        def _():
            send(column).start()

    def products(first, count):
        part = chunk(OUT, first, count)
        for k in range(first, first + count):
            pltpu.make_async_copy(s_ref.at[:, chunk(OUT, k)], s_ref.at[:, chunk(OUT, k)], f_recv.at[k]).wait()
        pair = table[PAIR, r * COLUMNS + column]
        last = first + count == len(OUT)

        def step(t, carry):
            grad_sq, pre_sq = carry
            rows = pl.ds(pl.multiple_of(t * TILE, TILE), TILE)
            middle = bf16(jnp.dot(l_ref[pair, rows, :], s_ref[:, part], preferred_element_type=jnp.float32))
            pre = jnp.dot(middle, r_ref[pair, part, :], preferred_element_type=jnp.float32)
            if first > 0:
                pre = pre + pf[rows, :]
            pf[rows, :] = pre
            grad_sq = grad_sq + jnp.sum(jnp.square(f32(s_ref[rows, part])), axis=0, keepdims=True)
            if last:
                pre_sq = pre_sq + jnp.sum(jnp.square(pre), axis=0, keepdims=True)
            return grad_sq, pre_sq

        zeros = (jnp.zeros((1, part.size), jnp.float32), jnp.zeros((1, SIDE), jnp.float32))
        grad_sq, pre_sq = lax.fori_loop(0, SIDE // TILE, step, zeros)
        return jnp.sum(grad_sq, axis=1, keepdims=True), jnp.sum(pre_sq, axis=1, keepdims=True)

    def hand_over(k):
        rows = d_ref.at[:, 1 - worker, :, chunk(BACK, k)]
        return pltpu.make_async_remote_copy(
            src_ref=rows, dst_ref=rows, send_sem=d_send.at[k], recv_sem=d_recv.at[k], device_id=(r, sibling),
            device_id_type=MESH,
        )

    def backward(k):
        ck = chunk(BACK, k)

        @pl.when(active)
        def _():
            factor = factor_ref[...]

            def scale(t, _):
                part = pf[pl.ds(pl.multiple_of(t * 128, 128), 128), ck] * factor
                d_ref[pl.ds(t * 4, 4), :, :, ck] = bf16(part).reshape(4, 2, ROWS, BACK[k])
                return 0

            lax.fori_loop(0, SIDE // 128, scale, 0)
            hand_over(k).start()

        @pl.when(idle)
        def _():
            hand_over(k).wait_recv()

        def step(n, _):
            q = offset(n)
            pltpu.make_async_remote_copy(
                src_ref=d_ref.at[q, c, :, ck], dst_ref=back[k].at[column], send_sem=b_send, recv_sem=b_recv.at[k],
                device_id=(r, 2 * q + c), device_id_type=MESH,
            ).start()
            return 0

        lax.fori_loop(0, COLUMNS - 1, step, 0)
        pltpu.make_async_copy(d_ref.at[column, c, :, ck], back[k].at[column], b_recv.at[k]).start()

    def gather_copies(k):
        n = 6 * k

        def spread(m, plane, half, to):
            part = fin[k].at[half_of(plane, half)]
            return remote(n + m, part, part, ag_send, ag_recv, to)

        return (
            spread(0, r, 0, up), spread(1, r, 1, dn), spread(2, r, 1, up), spread(3, r, 0, dn), spread(4, dn, 0, up),
            spread(5, up, 1, dn),
        )

    gathers = [gather_copies(k) for k in range(len(BACK))]

    def gather_first(k):
        pltpu.make_async_copy(back[k], back[k], b_recv.at[k]).wait()

        def place(i, _):
            e = r * SHARE + i
            fin[k][e] = back[k][table[COLUMN_OF, e]]
            return 0

        lax.fori_loop(0, SHARE, place, 0, unroll=4)
        for copy in gathers[k][:4]:
            copy.start()

    def gather_second(k):
        gathers[k][0].wait_recv()
        gathers[k][4].start()
        gathers[k][1].wait_recv()
        gathers[k][5].start()

    def finish(k):
        ck = chunk(BACK, k)
        for copy in gathers[k][2:]:
            copy.wait_recv()

        def place(b, _):
            o[b, :, ck] = fin[k][table[ENTRY_OF, b]]
            return 0

        lax.fori_loop(0, BLOCKS, place, 0, unroll=4)

    load_g.wait()
    load_table.wait()
    sum_first(0)

    @pl.when(active)
    def _():
        load_l.start()
        load_r.start()

    @pl.when(idle)
    def _():
        give_l.start()
        give_r.start()

    sum_second(0)
    sum_first(1)
    pl.semaphore_wait(plane_sem, 7)
    for k in range(len(OUT)):
        forward(k)
        if k + 1 < len(OUT):
            sum_second(k + 1)
        if k + 2 < len(OUT):
            sum_first(k + 2)

    @pl.when(active)
    def _():
        load_l.wait()
        load_r.wait()
        give_l.wait_recv()
        give_r.wait_recv()
        grad_ms, pre_sq = jnp.zeros((1, 1), jnp.float32), None
        for first, count in PARTS:
            grad_sq, pre_sq = products(first, count)
            grad_ms = grad_ms + grad_sq / (SIDE * SIDE)
        pre_ms = pre_sq / (SIDE * SIDE)
        factor_ref[...] = jnp.sqrt(grad_ms) * lax.rsqrt(pre_ms + EPSILON)

    for k in range(len(BACK) + 3):
        if k < len(BACK):
            backward(k)
        if 1 <= k <= len(BACK):
            gather_first(k - 1)
        if 2 <= k <= len(BACK) + 1:
            gather_second(k - 2)
        if k >= 3:
            finish(k - 3)

    for copies in sums + gathers:
        for copy in copies:
            copy.wait_send()

    sent = d_ref.at[pl.ds(1, COLUMNS - 1), 0]
    pltpu.make_async_copy(sent, sent, b_send).wait()

    @pl.when(active)
    def _():
        sent = outgoing.at[pl.ds(1, COLUMNS - 1)]
        pltpu.make_async_copy(sent, sent, f_send).wait()
        for k in range(len(BACK)):
            hand_over(k).wait_send()

    @pl.when(idle)
    def _():
        pltpu.make_async_copy(outgoing, outgoing, f_send).wait()
        give_l.wait_send()
        give_r.wait_send()


def on_device(grads, block_owner, left_roots, right_roots):
    anywhere = pl.BlockSpec(memory_space=pltpu.HBM)
    share = pltpu.VMEM((SHARE, ROWS, SIDE), jnp.bfloat16)
    half = pltpu.VMEM((HALF, ROWS, SIDE), jnp.bfloat16)
    column = pltpu.VMEM((COLUMNS, ROWS, SIDE), jnp.bfloat16)
    whole = pltpu.VMEM((BLOCKS, ROWS, SIDE), jnp.bfloat16)
    square = pltpu.VMEM((SIDE, SIDE), jnp.bfloat16)
    roots = pltpu.VMEM((4, SIDE, SIDE), jnp.bfloat16)
    dma = pltpu.SemaphoreType.DMA
    return pl.pallas_call(
        kernel,
        out_shape=jax.ShapeDtypeStruct((BLOCKS, ROWS, SIDE), jnp.bfloat16),
        in_specs=[pl.BlockSpec(memory_space=pltpu.SMEM), anywhere, anywhere, anywhere],
        out_specs=pl.BlockSpec(memory_space=pltpu.VMEM),
        scratch_shapes=[
            pltpu.VMEM((BLOCKS, 128), jnp.int32), pltpu.VMEM((8, 128), jnp.int32), pltpu.SMEM((8, 128), jnp.int32),
            whole, whole, half, half, half, half, share, share, share, column, square, roots, roots,
            pltpu.VMEM((SIDE, SIDE), jnp.float32), pltpu.VMEM((1, 1), jnp.float32), pltpu.VMEM((COLUMNS, 2, ROWS, SIDE), jnp.bfloat16),
            dma((4,)), dma((2,)), dma((2,)), dma((6 * len(OUT),)), dma((6 * len(OUT),)), dma, dma((len(OUT),)), dma, dma((len(BACK),)),
            dma((len(BACK),)), dma((len(BACK),)), dma((6 * len(BACK),)), dma((6 * len(BACK),)), pltpu.SemaphoreType.REGULAR,
            *[pltpu.VMEM((COLUMNS, ROWS, width), jnp.bfloat16) for width in BACK],
            *[pltpu.VMEM((BLOCKS, ROWS, width), jnp.bfloat16) for width in BACK],
        ],
        compiler_params=pltpu.CompilerParams(
            collective_id=0, has_side_effects=True, vmem_limit_bytes=51 * 1024 * 1024
        ),
        cost_estimate=pl.CostEstimate(flops=4 * SIDE**3, bytes_accessed=12 * 1024 * 1024, transcendentals=0),
    )(block_owner, grads, left_roots, right_roots)


def solution(mesh):
    in_specs = (P("replica", None, "fsdp", None), P(), P("fsdp", None, None), P("fsdp", None, None))
    return jax.shard_map(
        on_device, mesh=mesh, in_specs=in_specs, out_specs=P(None, "fsdp", None), check_vma=False
    )
```

```python
import jax
import jax.numpy as jnp
from jax import lax
from jax.experimental import pallas as pl
from jax.experimental.pallas import tpu as pltpu
from jax.sharding import PartitionSpec as P

EPSILON = 1e-06
MESH = pl.DeviceIdType.MESH

NY, NZ, NX = 4, 8, 4
COLUMNS = NZ * NX
BLOCKS = 64
SHARE = BLOCKS // NY
HALF = SHARE // 2
ROWS = 16
SIDE = 1024
OUT = (256, 256, 256, 256)
BACK = (256, 256, 256, 256)
PARTS = ((0, 2), (2, 1), (3, 1))
TILE = 1024

BLOCK_OF, ENTRY_OF, CELL, PAIR, COLUMN_OF = range(5)


def rem(a, b):
    return lax.rem(a, jnp.int32(b))


def div(a, b):
    return lax.div(a, jnp.int32(b))


def chunk(widths, k, count=1):
    return pl.ds(sum(widths[:k]), sum(widths[k : k + count]))


def f32(a):
    return a.astype(jnp.float32)


def bf16(a):
    return a.astype(jnp.bfloat16)


def make_table(owner, owners, table):
    lane1 = lax.broadcasted_iota(jnp.int32, (1, 128), 1)

    def spread(b, row):
        value = owner[b]
        owners[pl.ds(b, 1), :] = jnp.full((1, 128), value, jnp.int32)
        return jnp.where(lane1 == b, value, row)

    across = lax.fori_loop(0, BLOCKS, spread, jnp.full((1, 128), 4096, jnp.int32))
    down = owners[...]
    lane = lax.broadcasted_iota(jnp.int32, (BLOCKS, 128), 1)
    sub = lax.broadcasted_iota(jnp.int32, (BLOCKS, 128), 0)
    one, zero = jnp.ones((BLOCKS, 128), jnp.int32), jnp.zeros((BLOCKS, 128), jnp.int32)
    same = down == across
    earlier = jnp.logical_and(same, lane < sub)
    place = jnp.sum(jnp.where(jnp.logical_or(across < down, earlier), one, zero), axis=1, keepdims=True)
    slot = jnp.sum(jnp.where(earlier, one, zero), axis=1, keepdims=True)
    later = jnp.logical_or(down < across, jnp.logical_and(same, sub < lane))
    place_across = jnp.sum(jnp.where(later, one, zero), axis=0, keepdims=True)
    plane, position = place & 3, place >> 2
    column = down >> 1
    entry = jnp.where(plane * SHARE + position == lane, one, zero)
    here = jnp.where(jnp.logical_and(plane == (lane >> 5), column == (lane & 31)), one, zero)
    block = jnp.sum(entry * sub, axis=0, keepdims=True)
    cell = jnp.sum(here * position, axis=0, keepdims=True)
    pair = jnp.sum(here * (2 * (down & 1) + slot), axis=0, keepdims=True)
    column_of = jnp.sum(entry * column, axis=0, keepdims=True)
    table[pl.ds(BLOCK_OF, 1), :] = block & (BLOCKS - 1)
    table[pl.ds(ENTRY_OF, 1), :] = ((place_across & 3) * SHARE + (place_across >> 2)) & (BLOCKS - 1)
    table[pl.ds(CELL, 1), :] = cell & (SHARE - 1)
    table[pl.ds(PAIR, 1), :] = pair & 3
    table[pl.ds(COLUMN_OF, 1), :] = column_of & (COLUMNS - 1)


def kernel(owner, g_hbm, l_hbm, r_hbm, o, owners, table_v, table, g, gs, ta, tb, ca, cb, ra, rb, summed, outgoing, s_ref,
           l_ref, r_ref, pf, factor_ref, d_ref, load_sem, pair_send, pair_recv, rs_send, rs_recv, f_send, f_recv, b_send,
           b_recv, d_send, d_recv, ag_send, ag_recv, plane_sem, *by_chunk):
    back, fin = by_chunk[: len(BACK)], by_chunk[len(BACK) :]
    r, f = lax.axis_index("replica"), lax.axis_index("fsdp")
    z, x, c = div(f, 8), rem(div(f, 2), NX), rem(f, 2)
    in_line = rem(f, 8)
    column = div(f, 2)
    worker = rem(r, 2)
    active = worker == c
    idle = jnp.logical_not(active)
    sibling = f + 1 - 2 * c

    load_g = pltpu.make_async_copy(g_hbm.at[0], g, load_sem.at[0])
    load_g.start()

    def z_peer(d):
        return (r, rem(z + d, NZ) * 8 + in_line)

    barrier = pltpu.get_barrier_semaphore()
    for d in range(1, NY):
        pl.semaphore_signal(barrier, inc=1, device_id=(rem(r + d, NY), f), device_id_type=MESH)

    def greet(d, _):
        pl.semaphore_signal(barrier, inc=1, device_id=z_peer(d), device_id_type=MESH)
        pl.semaphore_signal(barrier, inc=1, device_id=(r, z * 8 + rem(in_line + d, 8)), device_id_type=MESH)
        return 0

    lax.fori_loop(1, 8, greet, 0)

    make_table(owner, owners, table_v)
    load_table = pltpu.make_async_copy(table_v, table, load_sem.at[1])
    load_table.start()

    own_pairs = pl.ds(2 * c, 2)
    load_l = pltpu.make_async_copy(l_hbm, l_ref.at[own_pairs], load_sem.at[2])
    load_r = pltpu.make_async_copy(r_hbm, r_ref.at[own_pairs], load_sem.at[3])

    def give(n, src, dst):
        return pltpu.make_async_remote_copy(
            src_ref=src, dst_ref=dst.at[own_pairs], send_sem=pair_send.at[n], recv_sem=pair_recv.at[n],
            device_id=(r, sibling), device_id_type=MESH,
        )

    give_l, give_r = give(0, l_hbm, l_ref), give(1, r_hbm, r_ref)

    up, dn, opp = rem(r + 1, NY), rem(r + 3, NY), rem(r + 2, NY)
    low, high = pl.ds(0, HALF), pl.ds(HALF, HALF)

    def half_of(plane, n):
        return pl.ds(plane * SHARE + n * HALF, HALF)

    def remote(n, src, dst, send, recv, plane):
        return pltpu.make_async_remote_copy(
            src_ref=src, dst_ref=dst, send_sem=send.at[n], recv_sem=recv.at[n], device_id=(plane, f), device_id_type=MESH
        )

    def sum_copies(k):
        ck, n = chunk(OUT, k), 6 * k
        return (
            remote(n, gs.at[half_of(opp, 0), :, ck], ta.at[:, :, ck], rs_send, rs_recv, up),
            remote(n + 1, gs.at[half_of(opp, 1), :, ck], tb.at[:, :, ck], rs_send, rs_recv, dn),
            remote(n + 2, gs.at[half_of(up, 1), :, ck], ra.at[high, :, ck], rs_send, rs_recv, up),
            remote(n + 3, gs.at[half_of(dn, 0), :, ck], rb.at[low, :, ck], rs_send, rs_recv, dn),
            remote(n + 4, ca.at[:, :, ck], ra.at[low, :, ck], rs_send, rs_recv, up),
            remote(n + 5, cb.at[:, :, ck], rb.at[high, :, ck], rs_send, rs_recv, dn),
        )

    sums = [sum_copies(k) for k in range(len(OUT))]

    def sum_pack(k):
        ck = chunk(OUT, k)

        def pack(e, _):
            gs[e, :, ck] = g[table[BLOCK_OF, e], :, ck]
            return 0

        lax.fori_loop(0, BLOCKS, pack, 0, unroll=4)

    def sum_first(k):
        for copy in sums[k][:4]:
            copy.start()

    def sum_far(k):
        sum_pack(k)
        for copy in sums[k][:2]:
            copy.start()

    def sum_near(k):
        for copy in sums[k][2:4]:
            copy.start()

    def sum_second(k):
        ck = chunk(OUT, k)

        def add_up(i, _):
            ca[i, :, ck] = bf16(f32(gs[up * SHARE + i, :, ck]) + f32(ta[i, :, ck]))
            return 0

        def add_dn(i, _):
            cb[i, :, ck] = bf16(f32(gs[dn * SHARE + HALF + i, :, ck]) + f32(tb[i, :, ck]))
            return 0

        sums[k][0].wait_recv()
        lax.fori_loop(0, HALF, add_up, 0, unroll=4)
        sums[k][4].start()
        sums[k][1].wait_recv()
        lax.fori_loop(0, HALF, add_dn, 0, unroll=4)
        sums[k][5].start()

    def offset(n):
        def step(i, size):
            return rem(size // 2 + div(i + 1, 2) * (1 - 2 * rem(i, 2)), size)

        return rem(z + step(div(n, NX), NZ), NZ) * NX + rem(x + step(rem(n, NX), NX), NX)

    def rows_of(rank):
        return pl.ds(pl.multiple_of(rank * ROWS, ROWS), ROWS)

    def forward(k):
        ck = chunk(OUT, k)
        for copy in sums[k][2:]:
            copy.wait_recv()

        def add(i, _):
            total = f32(gs[r * SHARE + i, :, ck]) + f32(ra[i, :, ck]) + f32(rb[i, :, ck])
            summed[i, :, ck] = bf16(total)
            return 0

        lax.fori_loop(0, SHARE, add, 0, unroll=4)

        def pack(q):
            outgoing[q, :, ck] = summed[table[CELL, r * COLUMNS + q], :, ck]

        def send(q):
            return pltpu.make_async_remote_copy(
                src_ref=outgoing.at[q, :, ck], dst_ref=s_ref.at[rows_of(f), ck], send_sem=f_send, recv_sem=f_recv.at[k],
                device_id=(r, 2 * q + worker), device_id_type=MESH,
            )

        def step(n, _):
            q = offset(n)
            pack(q)
            send(q).start()
            return 0

        lax.fori_loop(0, COLUMNS - 1, step, 0)
        pack(column)

        @pl.when(active)
        def _():
            pltpu.make_async_copy(outgoing.at[column, :, ck], s_ref.at[rows_of(f), ck], f_recv.at[k]).start()

        @pl.when(idle)
        def _():
            send(column).start()

    def products(first, count):
        part = chunk(OUT, first, count)
        for k in range(first, first + count):
            pltpu.make_async_copy(s_ref.at[:, chunk(OUT, k)], s_ref.at[:, chunk(OUT, k)], f_recv.at[k]).wait()
        pair = table[PAIR, r * COLUMNS + column]
        last = first + count == len(OUT)

        def step(t, carry):
            grad_sq, pre_sq = carry
            rows = pl.ds(pl.multiple_of(t * TILE, TILE), TILE)
            middle = bf16(jnp.dot(l_ref[pair, rows, :], s_ref[:, part], preferred_element_type=jnp.float32))
            pre = jnp.dot(middle, r_ref[pair, part, :], preferred_element_type=jnp.float32)
            if first > 0:
                pre = pre + pf[rows, :]
            pf[rows, :] = pre
            grad_sq = grad_sq + jnp.sum(jnp.square(f32(s_ref[rows, part])), axis=0, keepdims=True)
            if last:
                pre_sq = pre_sq + jnp.sum(jnp.square(pre), axis=0, keepdims=True)
            return grad_sq, pre_sq

        zeros = (jnp.zeros((1, part.size), jnp.float32), jnp.zeros((1, SIDE), jnp.float32))
        grad_sq, pre_sq = lax.fori_loop(0, SIDE // TILE, step, zeros)
        return jnp.sum(grad_sq, axis=1, keepdims=True), jnp.sum(pre_sq, axis=1, keepdims=True)

    def hand_over(k):
        rows = d_ref.at[:, 1 - worker, :, chunk(BACK, k)]
        return pltpu.make_async_remote_copy(
            src_ref=rows, dst_ref=rows, send_sem=d_send.at[k], recv_sem=d_recv.at[k], device_id=(r, sibling),
            device_id_type=MESH,
        )

    def backward(k):
        ck = chunk(BACK, k)

        @pl.when(active)
        def _():
            factor = factor_ref[...]

            def scale(t, _):
                part = pf[pl.ds(pl.multiple_of(t * 128, 128), 128), ck] * factor
                d_ref[pl.ds(t * 4, 4), :, :, ck] = bf16(part).reshape(4, 2, ROWS, BACK[k])
                return 0

            lax.fori_loop(0, SIDE // 128, scale, 0, unroll=4)
            hand_over(k).start()

        @pl.when(idle)
        def _():
            hand_over(k).wait_recv()

        def step(n, _):
            q = offset(n)
            pltpu.make_async_remote_copy(
                src_ref=d_ref.at[q, c, :, ck], dst_ref=back[k].at[column], send_sem=b_send, recv_sem=b_recv.at[k],
                device_id=(r, 2 * q + c), device_id_type=MESH,
            ).start()
            return 0

        lax.fori_loop(0, COLUMNS - 1, step, 0)
        pltpu.make_async_copy(d_ref.at[column, c, :, ck], back[k].at[column], b_recv.at[k]).start()

    def gather_copies(k):
        n = 6 * k

        def spread(m, plane, half, to):
            part = fin[k].at[half_of(plane, half)]
            return remote(n + m, part, part, ag_send, ag_recv, to)

        return (
            spread(0, r, 0, up), spread(1, r, 1, dn), spread(2, r, 1, up), spread(3, r, 0, dn), spread(4, dn, 0, up),
            spread(5, up, 1, dn),
        )

    gathers = [gather_copies(k) for k in range(len(BACK))]

    def gather_first(k):
        pltpu.make_async_copy(back[k], back[k], b_recv.at[k]).wait()

        def place(i, _):
            e = r * SHARE + i
            fin[k][e] = back[k][table[COLUMN_OF, e]]
            return 0

        lax.fori_loop(0, SHARE, place, 0, unroll=4)
        for copy in gathers[k][:4]:
            copy.start()

    def gather_second(k):
        gathers[k][0].wait_recv()
        gathers[k][4].start()
        gathers[k][1].wait_recv()
        gathers[k][5].start()

    def finish(k):
        ck = chunk(BACK, k)
        for copy in gathers[k][2:]:
            copy.wait_recv()

        def place(b, _):
            o[b, :, ck] = fin[k][table[ENTRY_OF, b]]
            return 0

        lax.fori_loop(0, BLOCKS, place, 0, unroll=4)

    load_g.wait()
    load_table.wait()
    sum_pack(0)
    pl.semaphore_wait(barrier, 17)
    sum_first(0)

    def greet_plane(d, _):
        pl.semaphore_signal(plane_sem, inc=1, device_id=z_peer(d), device_id_type=MESH)
        return 0

    lax.fori_loop(1, 8, greet_plane, 0)

    @pl.when(active)
    def _():
        load_l.start()
        load_r.start()

    @pl.when(idle)
    def _():
        give_l.start()
        give_r.start()

    sum_second(0)
    sum_pack(1)
    sum_first(1)
    pl.semaphore_wait(plane_sem, 7)
    forward(0)
    sum_second(1)
    sum_pack(2)
    sum_first(2)
    forward(1)
    sum_second(2)
    sum_pack(3)
    sum_first(3)
    forward(2)
    sum_second(3)
    forward(3)

    @pl.when(active)
    def _():
        load_l.wait()
        load_r.wait()
        give_l.wait_recv()
        give_r.wait_recv()
        grad_ms, pre_sq = jnp.zeros((1, 1), jnp.float32), None
        for first, count in PARTS:
            grad_sq, pre_sq = products(first, count)
            grad_ms = grad_ms + grad_sq / (SIDE * SIDE)
        pre_ms = pre_sq / (SIDE * SIDE)
        factor_ref[...] = jnp.sqrt(grad_ms) * lax.rsqrt(pre_ms + EPSILON)

    for k in range(len(BACK) + 3):
        if k < len(BACK):
            backward(k)
        if 1 <= k <= len(BACK):
            gather_first(k - 1)
        if 2 <= k <= len(BACK) + 1:
            gather_second(k - 2)
        if k >= 3:
            finish(k - 3)

    for copies in sums + gathers:
        for copy in copies:
            copy.wait_send()

    sent = d_ref.at[pl.ds(1, COLUMNS - 1), 0]
    pltpu.make_async_copy(sent, sent, b_send).wait()

    @pl.when(active)
    def _():
        sent = outgoing.at[pl.ds(1, COLUMNS - 1)]
        pltpu.make_async_copy(sent, sent, f_send).wait()
        for k in range(len(BACK)):
            hand_over(k).wait_send()

    @pl.when(idle)
    def _():
        pltpu.make_async_copy(outgoing, outgoing, f_send).wait()
        give_l.wait_send()
        give_r.wait_send()


def on_device(grads, block_owner, left_roots, right_roots):
    anywhere = pl.BlockSpec(memory_space=pltpu.HBM)
    share = pltpu.VMEM((SHARE, ROWS, SIDE), jnp.bfloat16)
    half = pltpu.VMEM((HALF, ROWS, SIDE), jnp.bfloat16)
    column = pltpu.VMEM((COLUMNS, ROWS, SIDE), jnp.bfloat16)
    whole = pltpu.VMEM((BLOCKS, ROWS, SIDE), jnp.bfloat16)
    square = pltpu.VMEM((SIDE, SIDE), jnp.bfloat16)
    roots = pltpu.VMEM((4, SIDE, SIDE), jnp.bfloat16)
    dma = pltpu.SemaphoreType.DMA
    return pl.pallas_call(
        kernel,
        out_shape=jax.ShapeDtypeStruct((BLOCKS, ROWS, SIDE), jnp.bfloat16),
        in_specs=[pl.BlockSpec(memory_space=pltpu.SMEM), anywhere, anywhere, anywhere],
        out_specs=pl.BlockSpec(memory_space=pltpu.VMEM),
        scratch_shapes=[
            pltpu.VMEM((BLOCKS, 128), jnp.int32), pltpu.VMEM((8, 128), jnp.int32), pltpu.SMEM((8, 128), jnp.int32),
            whole, whole, half, half, half, half, share, share, share, column, square, roots, roots,
            pltpu.VMEM((SIDE, SIDE), jnp.float32), pltpu.VMEM((1, 1), jnp.float32), pltpu.VMEM((COLUMNS, 2, ROWS, SIDE), jnp.bfloat16),
            dma((4,)), dma((2,)), dma((2,)), dma((6 * len(OUT),)), dma((6 * len(OUT),)), dma, dma((len(OUT),)), dma, dma((len(BACK),)),
            dma((len(BACK),)), dma((len(BACK),)), dma((6 * len(BACK),)), dma((6 * len(BACK),)), pltpu.SemaphoreType.REGULAR,
            *[pltpu.VMEM((COLUMNS, ROWS, width), jnp.bfloat16) for width in BACK],
            *[pltpu.VMEM((BLOCKS, ROWS, width), jnp.bfloat16) for width in BACK],
        ],
        compiler_params=pltpu.CompilerParams(
            collective_id=0, has_side_effects=True, vmem_limit_bytes=51 * 1024 * 1024
        ),
        cost_estimate=pl.CostEstimate(flops=4 * SIDE**3, bytes_accessed=12 * 1024 * 1024, transcendentals=0),
    )(block_owner, grads, left_roots, right_roots)


def solution(mesh):
    in_specs = (P("replica", None, "fsdp", None), P(), P("fsdp", None, None), P("fsdp", None, None))
    return jax.shard_map(
        on_device, mesh=mesh, in_specs=in_specs, out_specs=P(None, "fsdp", None), check_vma=False
    )
```

```python
import jax
import jax.numpy as jnp
from jax import lax
from jax.experimental import pallas as pl
from jax.experimental.pallas import tpu as pltpu
from jax.sharding import PartitionSpec as P

EPSILON = 1e-06
MESH = pl.DeviceIdType.MESH

NY, NZ, NX = 4, 8, 4
COLUMNS = NZ * NX
BLOCKS = 64
SHARE = BLOCKS // NY
HALF = SHARE // 2
ROWS = 16
SIDE = 1024
OUT = (256, 256, 256, 256)
BACK = (256, 256, 256, 256)
PARTS = ((0, 2), (2, 1), (3, 1))
TILE = 1024

BLOCK_OF, ENTRY_OF, CELL, PAIR, COLUMN_OF = range(5)


def rem(a, b):
    return lax.rem(a, jnp.int32(b))


def div(a, b):
    return lax.div(a, jnp.int32(b))


def chunk(widths, k, count=1):
    return pl.ds(sum(widths[:k]), sum(widths[k : k + count]))


def f32(a):
    return a.astype(jnp.float32)


def bf16(a):
    return a.astype(jnp.bfloat16)


def make_table(owner, owners, table):
    lane1 = lax.broadcasted_iota(jnp.int32, (1, 128), 1)

    def spread(b, row):
        value = owner[b]
        owners[pl.ds(b, 1), :] = jnp.full((1, 128), value, jnp.int32)
        return jnp.where(lane1 == b, value, row)

    across = lax.fori_loop(0, BLOCKS, spread, jnp.full((1, 128), 4096, jnp.int32))
    down = owners[...]
    lane = lax.broadcasted_iota(jnp.int32, (BLOCKS, 128), 1)
    sub = lax.broadcasted_iota(jnp.int32, (BLOCKS, 128), 0)
    one, zero = jnp.ones((BLOCKS, 128), jnp.int32), jnp.zeros((BLOCKS, 128), jnp.int32)
    same = down == across
    earlier = jnp.logical_and(same, lane < sub)
    place = jnp.sum(jnp.where(jnp.logical_or(across < down, earlier), one, zero), axis=1, keepdims=True)
    slot = jnp.sum(jnp.where(earlier, one, zero), axis=1, keepdims=True)
    later = jnp.logical_or(down < across, jnp.logical_and(same, sub < lane))
    place_across = jnp.sum(jnp.where(later, one, zero), axis=0, keepdims=True)
    plane, position = place & 3, place >> 2
    column = down >> 1
    entry = jnp.where(plane * SHARE + position == lane, one, zero)
    here = jnp.where(jnp.logical_and(plane == (lane >> 5), column == (lane & 31)), one, zero)
    block = jnp.sum(entry * sub, axis=0, keepdims=True)
    cell = jnp.sum(here * position, axis=0, keepdims=True)
    pair = jnp.sum(here * (2 * (down & 1) + slot), axis=0, keepdims=True)
    column_of = jnp.sum(entry * column, axis=0, keepdims=True)
    table[pl.ds(BLOCK_OF, 1), :] = block & (BLOCKS - 1)
    table[pl.ds(ENTRY_OF, 1), :] = ((place_across & 3) * SHARE + (place_across >> 2)) & (BLOCKS - 1)
    table[pl.ds(CELL, 1), :] = cell & (SHARE - 1)
    table[pl.ds(PAIR, 1), :] = pair & 3
    table[pl.ds(COLUMN_OF, 1), :] = column_of & (COLUMNS - 1)


def kernel(owner, g_hbm, l_hbm, r_hbm, o, owners, table_v, table, g, gs, ta, tb, ca, cb, ra, rb, summed, outgoing, s_ref,
           l_ref, r_ref, pf, factor_ref, d_ref, load_sem, pair_send, pair_recv, rs_send, rs_recv, f_send, f_recv, b_send,
           b_recv, d_send, d_recv, ag_send, ag_recv, plane_sem, *by_chunk):
    back, fin = by_chunk[: len(BACK)], by_chunk[len(BACK) :]
    r, f = lax.axis_index("replica"), lax.axis_index("fsdp")
    z, x, c = div(f, 8), rem(div(f, 2), NX), rem(f, 2)
    in_line = rem(f, 8)
    column = div(f, 2)
    worker = rem(r, 2)
    active = worker == c
    idle = jnp.logical_not(active)
    sibling = f + 1 - 2 * c

    load_g = pltpu.make_async_copy(g_hbm.at[0], g, load_sem.at[0])
    load_g.start()

    def z_peer(d):
        return (r, rem(z + d, NZ) * 8 + in_line)

    barrier = pltpu.get_barrier_semaphore()
    for d in range(1, NY):
        pl.semaphore_signal(barrier, inc=1, device_id=(rem(r + d, NY), f), device_id_type=MESH)

    def greet(d, _):
        pl.semaphore_signal(barrier, inc=1, device_id=z_peer(d), device_id_type=MESH)
        pl.semaphore_signal(barrier, inc=1, device_id=(r, z * 8 + rem(in_line + d, 8)), device_id_type=MESH)
        return 0

    lax.fori_loop(1, 8, greet, 0)

    make_table(owner, owners, table_v)
    load_table = pltpu.make_async_copy(table_v, table, load_sem.at[1])
    load_table.start()

    own_pairs = pl.ds(2 * c, 2)
    load_l = pltpu.make_async_copy(l_hbm, l_ref.at[own_pairs], load_sem.at[2])
    load_r = pltpu.make_async_copy(r_hbm, r_ref.at[own_pairs], load_sem.at[3])

    def give(n, src, dst):
        return pltpu.make_async_remote_copy(
            src_ref=src, dst_ref=dst.at[own_pairs], send_sem=pair_send.at[n], recv_sem=pair_recv.at[n],
            device_id=(r, sibling), device_id_type=MESH,
        )

    give_l, give_r = give(0, l_hbm, l_ref), give(1, r_hbm, r_ref)

    up, dn, opp = rem(r + 1, NY), rem(r + 3, NY), rem(r + 2, NY)
    low, high = pl.ds(0, HALF), pl.ds(HALF, HALF)

    def half_of(plane, n):
        return pl.ds(plane * SHARE + n * HALF, HALF)

    def remote(n, src, dst, send, recv, plane):
        return pltpu.make_async_remote_copy(
            src_ref=src, dst_ref=dst, send_sem=send.at[n], recv_sem=recv.at[n], device_id=(plane, f), device_id_type=MESH
        )

    def sum_copies(k):
        ck, n = chunk(OUT, k), 6 * k
        return (
            remote(n, gs.at[half_of(opp, 0), :, ck], ta.at[:, :, ck], rs_send, rs_recv, up),
            remote(n + 1, gs.at[half_of(opp, 1), :, ck], tb.at[:, :, ck], rs_send, rs_recv, dn),
            remote(n + 2, gs.at[half_of(up, 1), :, ck], ra.at[high, :, ck], rs_send, rs_recv, up),
            remote(n + 3, gs.at[half_of(dn, 0), :, ck], rb.at[low, :, ck], rs_send, rs_recv, dn),
            remote(n + 4, ca.at[:, :, ck], ra.at[low, :, ck], rs_send, rs_recv, up),
            remote(n + 5, cb.at[:, :, ck], rb.at[high, :, ck], rs_send, rs_recv, dn),
        )

    sums = [sum_copies(k) for k in range(len(OUT))]

    def sum_pack(k):
        ck = chunk(OUT, k)

        def pack(e, _):
            gs[e, :, ck] = g[table[BLOCK_OF, e], :, ck]
            return 0

        lax.fori_loop(0, BLOCKS, pack, 0, unroll=4)

    def sum_first(k):
        for copy in sums[k][:4]:
            copy.start()

    def sum_far(k):
        sum_pack(k)
        for copy in sums[k][:2]:
            copy.start()

    def sum_near(k):
        for copy in sums[k][2:4]:
            copy.start()

    def sum_second(k):
        ck = chunk(OUT, k)

        def add_up(i, _):
            ca[i, :, ck] = bf16(f32(gs[up * SHARE + i, :, ck]) + f32(ta[i, :, ck]))
            return 0

        def add_dn(i, _):
            cb[i, :, ck] = bf16(f32(gs[dn * SHARE + HALF + i, :, ck]) + f32(tb[i, :, ck]))
            return 0

        sums[k][0].wait_recv()
        lax.fori_loop(0, HALF, add_up, 0, unroll=4)
        sums[k][4].start()
        sums[k][1].wait_recv()
        lax.fori_loop(0, HALF, add_dn, 0, unroll=4)
        sums[k][5].start()

    def offset(n):
        def step(i, size):
            return rem(size // 2 + div(i + 1, 2) * (1 - 2 * rem(i, 2)), size)

        return rem(z + step(div(n, NX), NZ), NZ) * NX + rem(x + step(rem(n, NX), NX), NX)

    def rows_of(rank):
        return pl.ds(pl.multiple_of(rank * ROWS, ROWS), ROWS)

    def forward(k):
        ck = chunk(OUT, k)
        for copy in sums[k][2:]:
            copy.wait_recv()

        def add(i, _):
            total = f32(gs[r * SHARE + i, :, ck]) + f32(ra[i, :, ck]) + f32(rb[i, :, ck])
            summed[i, :, ck] = bf16(total)
            return 0

        lax.fori_loop(0, SHARE, add, 0, unroll=4)

        def pack(q):
            outgoing[q, :, ck] = summed[table[CELL, r * COLUMNS + q], :, ck]

        def send(q):
            return pltpu.make_async_remote_copy(
                src_ref=outgoing.at[q, :, ck], dst_ref=s_ref.at[rows_of(f), ck], send_sem=f_send, recv_sem=f_recv.at[k],
                device_id=(r, 2 * q + worker), device_id_type=MESH,
            )

        def step(n, _):
            q = offset(n)
            pack(q)
            send(q).start()
            return 0

        lax.fori_loop(0, COLUMNS - 1, step, 0, unroll=True)
        pack(column)

        @pl.when(active)
        def _():
            pltpu.make_async_copy(outgoing.at[column, :, ck], s_ref.at[rows_of(f), ck], f_recv.at[k]).start()

        @pl.when(idle)
        def _():
            send(column).start()

    def products(first, count):
        part = chunk(OUT, first, count)
        for k in range(first, first + count):
            pltpu.make_async_copy(s_ref.at[:, chunk(OUT, k)], s_ref.at[:, chunk(OUT, k)], f_recv.at[k]).wait()
        pair = table[PAIR, r * COLUMNS + column]
        last = first + count == len(OUT)

        def step(t, carry):
            grad_sq, pre_sq = carry
            rows = pl.ds(pl.multiple_of(t * TILE, TILE), TILE)
            middle = bf16(jnp.dot(l_ref[pair, rows, :], s_ref[:, part], preferred_element_type=jnp.float32))
            pre = jnp.dot(middle, r_ref[pair, part, :], preferred_element_type=jnp.float32)
            if first > 0:
                pre = pre + pf[rows, :]
            pf[rows, :] = pre
            grad_sq = grad_sq + jnp.sum(jnp.square(f32(s_ref[rows, part])), axis=0, keepdims=True)
            if last:
                pre_sq = pre_sq + jnp.sum(jnp.square(pre), axis=0, keepdims=True)
            return grad_sq, pre_sq

        zeros = (jnp.zeros((1, part.size), jnp.float32), jnp.zeros((1, SIDE), jnp.float32))
        grad_sq, pre_sq = lax.fori_loop(0, SIDE // TILE, step, zeros)
        return jnp.sum(grad_sq, axis=1, keepdims=True), jnp.sum(pre_sq, axis=1, keepdims=True)

    def hand_over(k):
        rows = d_ref.at[:, 1 - worker, :, chunk(BACK, k)]
        return pltpu.make_async_remote_copy(
            src_ref=rows, dst_ref=rows, send_sem=d_send.at[k], recv_sem=d_recv.at[k], device_id=(r, sibling),
            device_id_type=MESH,
        )

    def backward(k):
        ck = chunk(BACK, k)

        @pl.when(active)
        def _():
            factor = factor_ref[...]

            def scale(t, _):
                part = pf[pl.ds(pl.multiple_of(t * 128, 128), 128), ck] * factor
                d_ref[pl.ds(t * 4, 4), :, :, ck] = bf16(part).reshape(4, 2, ROWS, BACK[k])
                return 0

            lax.fori_loop(0, SIDE // 128, scale, 0, unroll=4)
            hand_over(k).start()

        @pl.when(idle)
        def _():
            hand_over(k).wait_recv()

        def step(n, _):
            q = offset(n)
            pltpu.make_async_remote_copy(
                src_ref=d_ref.at[q, c, :, ck], dst_ref=back[k].at[column], send_sem=b_send, recv_sem=b_recv.at[k],
                device_id=(r, 2 * q + c), device_id_type=MESH,
            ).start()
            return 0

        lax.fori_loop(0, COLUMNS - 1, step, 0, unroll=True)
        pltpu.make_async_copy(d_ref.at[column, c, :, ck], back[k].at[column], b_recv.at[k]).start()

    def gather_copies(k):
        n = 6 * k

        def spread(m, plane, half, to):
            part = fin[k].at[half_of(plane, half)]
            return remote(n + m, part, part, ag_send, ag_recv, to)

        return (
            spread(0, r, 0, up), spread(1, r, 1, dn), spread(2, r, 1, up), spread(3, r, 0, dn), spread(4, dn, 0, up),
            spread(5, up, 1, dn),
        )

    gathers = [gather_copies(k) for k in range(len(BACK))]

    def gather_first(k):
        pltpu.make_async_copy(back[k], back[k], b_recv.at[k]).wait()

        def place(i, _):
            e = r * SHARE + i
            fin[k][e] = back[k][table[COLUMN_OF, e]]
            return 0

        lax.fori_loop(0, SHARE, place, 0, unroll=4)
        for copy in gathers[k][:4]:
            copy.start()

    def gather_second(k):
        gathers[k][0].wait_recv()
        gathers[k][4].start()
        gathers[k][1].wait_recv()
        gathers[k][5].start()

    def finish(k):
        ck = chunk(BACK, k)
        for copy in gathers[k][2:]:
            copy.wait_recv()

        def place(b, _):
            o[b, :, ck] = fin[k][table[ENTRY_OF, b]]
            return 0

        lax.fori_loop(0, BLOCKS, place, 0, unroll=4)

    load_g.wait()
    load_table.wait()
    sum_pack(0)
    pl.semaphore_wait(barrier, 17)
    sum_first(0)

    def greet_plane(d, _):
        pl.semaphore_signal(plane_sem, inc=1, device_id=z_peer(d), device_id_type=MESH)
        return 0

    lax.fori_loop(1, 8, greet_plane, 0)

    @pl.when(active)
    def _():
        load_l.start()
        load_r.start()

    @pl.when(idle)
    def _():
        give_l.start()
        give_r.start()

    sum_second(0)
    sum_pack(1)
    sum_first(1)
    pl.semaphore_wait(plane_sem, 7)
    forward(0)
    sum_second(1)
    sum_pack(2)
    sum_first(2)
    forward(1)
    sum_second(2)
    sum_pack(3)
    sum_first(3)
    forward(2)
    sum_second(3)
    forward(3)

    @pl.when(active)
    def _():
        load_l.wait()
        load_r.wait()
        give_l.wait_recv()
        give_r.wait_recv()
        grad_ms, pre_sq = jnp.zeros((1, 1), jnp.float32), None
        for first, count in PARTS:
            grad_sq, pre_sq = products(first, count)
            grad_ms = grad_ms + grad_sq / (SIDE * SIDE)
        pre_ms = pre_sq / (SIDE * SIDE)
        factor_ref[...] = jnp.sqrt(grad_ms) * lax.rsqrt(pre_ms + EPSILON)

    for k in range(len(BACK) + 3):
        if k < len(BACK):
            backward(k)
        if 1 <= k <= len(BACK):
            gather_first(k - 1)
        if 2 <= k <= len(BACK) + 1:
            gather_second(k - 2)
        if k >= 3:
            finish(k - 3)

    for copies in sums + gathers:
        for copy in copies:
            copy.wait_send()

    sent = d_ref.at[pl.ds(1, COLUMNS - 1), 0]
    pltpu.make_async_copy(sent, sent, b_send).wait()

    @pl.when(active)
    def _():
        sent = outgoing.at[pl.ds(1, COLUMNS - 1)]
        pltpu.make_async_copy(sent, sent, f_send).wait()
        for k in range(len(BACK)):
            hand_over(k).wait_send()

    @pl.when(idle)
    def _():
        pltpu.make_async_copy(outgoing, outgoing, f_send).wait()
        give_l.wait_send()
        give_r.wait_send()


def on_device(grads, block_owner, left_roots, right_roots):
    anywhere = pl.BlockSpec(memory_space=pltpu.HBM)
    share = pltpu.VMEM((SHARE, ROWS, SIDE), jnp.bfloat16)
    half = pltpu.VMEM((HALF, ROWS, SIDE), jnp.bfloat16)
    column = pltpu.VMEM((COLUMNS, ROWS, SIDE), jnp.bfloat16)
    whole = pltpu.VMEM((BLOCKS, ROWS, SIDE), jnp.bfloat16)
    square = pltpu.VMEM((SIDE, SIDE), jnp.bfloat16)
    roots = pltpu.VMEM((4, SIDE, SIDE), jnp.bfloat16)
    dma = pltpu.SemaphoreType.DMA
    return pl.pallas_call(
        kernel,
        out_shape=jax.ShapeDtypeStruct((BLOCKS, ROWS, SIDE), jnp.bfloat16),
        in_specs=[pl.BlockSpec(memory_space=pltpu.SMEM), anywhere, anywhere, anywhere],
        out_specs=pl.BlockSpec(memory_space=pltpu.VMEM),
        scratch_shapes=[
            pltpu.VMEM((BLOCKS, 128), jnp.int32), pltpu.VMEM((8, 128), jnp.int32), pltpu.SMEM((8, 128), jnp.int32),
            whole, whole, half, half, half, half, share, share, share, column, square, roots, roots,
            pltpu.VMEM((SIDE, SIDE), jnp.float32), pltpu.VMEM((1, 1), jnp.float32), pltpu.VMEM((COLUMNS, 2, ROWS, SIDE), jnp.bfloat16),
            dma((4,)), dma((2,)), dma((2,)), dma((6 * len(OUT),)), dma((6 * len(OUT),)), dma, dma((len(OUT),)), dma, dma((len(BACK),)),
            dma((len(BACK),)), dma((len(BACK),)), dma((6 * len(BACK),)), dma((6 * len(BACK),)), pltpu.SemaphoreType.REGULAR,
            *[pltpu.VMEM((COLUMNS, ROWS, width), jnp.bfloat16) for width in BACK],
            *[pltpu.VMEM((BLOCKS, ROWS, width), jnp.bfloat16) for width in BACK],
        ],
        compiler_params=pltpu.CompilerParams(
            collective_id=0, has_side_effects=True, vmem_limit_bytes=51 * 1024 * 1024
        ),
        cost_estimate=pl.CostEstimate(flops=4 * SIDE**3, bytes_accessed=12 * 1024 * 1024, transcendentals=0),
    )(block_owner, grads, left_roots, right_roots)


def solution(mesh):
    in_specs = (P("replica", None, "fsdp", None), P(), P("fsdp", None, None), P("fsdp", None, None))
    return jax.shard_map(
        on_device, mesh=mesh, in_specs=in_specs, out_specs=P(None, "fsdp", None), check_vma=False
    )
```

```python
import jax
import jax.numpy as jnp
from jax import lax
from jax.experimental import pallas as pl
from jax.experimental.pallas import tpu as pltpu
from jax.sharding import PartitionSpec as P

EPSILON = 1e-06
MESH = pl.DeviceIdType.MESH

NY, NZ, NX = 4, 8, 4
COLUMNS = NZ * NX
BLOCKS = 64
SHARE = BLOCKS // NY
HALF = SHARE // 2
ROWS = 16
SIDE = 1024
OUT = (256, 256, 256, 256)
BACK = (256, 256, 256, 256)
PARTS = ((0, 2), (2, 1), (3, 1))
TILE = 1024

BLOCK_OF, ENTRY_OF, CELL, PAIR, COLUMN_OF = range(5)


def rem(a, b):
    return lax.rem(a, jnp.int32(b))


def div(a, b):
    return lax.div(a, jnp.int32(b))


def chunk(widths, k, count=1):
    return pl.ds(sum(widths[:k]), sum(widths[k : k + count]))


def f32(a):
    return a.astype(jnp.float32)


def bf16(a):
    return a.astype(jnp.bfloat16)


def make_table(owner, owners, table):
    lane1 = lax.broadcasted_iota(jnp.int32, (1, 128), 1)

    def spread(b, row):
        value = owner[b]
        owners[pl.ds(b, 1), :] = jnp.full((1, 128), value, jnp.int32)
        return jnp.where(lane1 == b, value, row)

    across = lax.fori_loop(0, BLOCKS, spread, jnp.full((1, 128), 4096, jnp.int32))
    down = owners[...]
    lane = lax.broadcasted_iota(jnp.int32, (BLOCKS, 128), 1)
    sub = lax.broadcasted_iota(jnp.int32, (BLOCKS, 128), 0)
    one, zero = jnp.ones((BLOCKS, 128), jnp.int32), jnp.zeros((BLOCKS, 128), jnp.int32)
    same = down == across
    earlier = jnp.logical_and(same, lane < sub)
    place = jnp.sum(jnp.where(jnp.logical_or(across < down, earlier), one, zero), axis=1, keepdims=True)
    slot = jnp.sum(jnp.where(earlier, one, zero), axis=1, keepdims=True)
    later = jnp.logical_or(down < across, jnp.logical_and(same, sub < lane))
    place_across = jnp.sum(jnp.where(later, one, zero), axis=0, keepdims=True)
    plane, position = place & 3, place >> 2
    column = down >> 1
    entry = jnp.where(plane * SHARE + position == lane, one, zero)
    here = jnp.where(jnp.logical_and(plane == (lane >> 5), column == (lane & 31)), one, zero)
    block = jnp.sum(entry * sub, axis=0, keepdims=True)
    cell = jnp.sum(here * position, axis=0, keepdims=True)
    pair = jnp.sum(here * (2 * (down & 1) + slot), axis=0, keepdims=True)
    column_of = jnp.sum(entry * column, axis=0, keepdims=True)
    table[pl.ds(BLOCK_OF, 1), :] = block & (BLOCKS - 1)
    table[pl.ds(ENTRY_OF, 1), :] = ((place_across & 3) * SHARE + (place_across >> 2)) & (BLOCKS - 1)
    table[pl.ds(CELL, 1), :] = cell & (SHARE - 1)
    table[pl.ds(PAIR, 1), :] = pair & 3
    table[pl.ds(COLUMN_OF, 1), :] = column_of & (COLUMNS - 1)


def kernel(owner, g_hbm, l_hbm, r_hbm, o, owners, table_v, table, g, gs, ta, tb, ca, cb, ra, rb, summed, outgoing, s_ref,
           l_ref, r_ref, pf, factor_ref, d_ref, load_sem, pair_send, pair_recv, rs_send, rs_recv, f_send, f_recv, b_send,
           b_recv, d_send, d_recv, ag_send, ag_recv, plane_sem, *by_chunk):
    back, fin = by_chunk[: len(BACK)], by_chunk[len(BACK) :]
    r, f = lax.axis_index("replica"), lax.axis_index("fsdp")
    z, x, c = div(f, 8), rem(div(f, 2), NX), rem(f, 2)
    in_line = rem(f, 8)
    column = div(f, 2)
    worker = rem(r, 2)
    active = worker == c
    idle = jnp.logical_not(active)
    sibling = f + 1 - 2 * c

    load_g = pltpu.make_async_copy(g_hbm.at[0], g, load_sem.at[0])
    load_g.start()

    def z_peer(d):
        return (r, rem(z + d, NZ) * 8 + in_line)

    barrier = pltpu.get_barrier_semaphore()
    for d in range(1, NY):
        pl.semaphore_signal(barrier, inc=1, device_id=(rem(r + d, NY), f), device_id_type=MESH)

    def greet(d, _):
        pl.semaphore_signal(barrier, inc=1, device_id=z_peer(d), device_id_type=MESH)
        pl.semaphore_signal(barrier, inc=1, device_id=(r, z * 8 + rem(in_line + d, 8)), device_id_type=MESH)
        return 0

    lax.fori_loop(1, 8, greet, 0)

    make_table(owner, owners, table_v)
    load_table = pltpu.make_async_copy(table_v, table, load_sem.at[1])
    load_table.start()

    own_pairs = pl.ds(2 * c, 2)
    load_l = pltpu.make_async_copy(l_hbm, l_ref.at[own_pairs], load_sem.at[2])
    load_r = pltpu.make_async_copy(r_hbm, r_ref.at[own_pairs], load_sem.at[3])

    def give(n, src, dst):
        return pltpu.make_async_remote_copy(
            src_ref=src, dst_ref=dst.at[own_pairs], send_sem=pair_send.at[n], recv_sem=pair_recv.at[n],
            device_id=(r, sibling), device_id_type=MESH,
        )

    give_l, give_r = give(0, l_hbm, l_ref), give(1, r_hbm, r_ref)

    up, dn, opp = rem(r + 1, NY), rem(r + 3, NY), rem(r + 2, NY)
    low, high = pl.ds(0, HALF), pl.ds(HALF, HALF)

    def half_of(plane, n):
        return pl.ds(plane * SHARE + n * HALF, HALF)

    def remote(n, src, dst, send, recv, plane):
        return pltpu.make_async_remote_copy(
            src_ref=src, dst_ref=dst, send_sem=send.at[n], recv_sem=recv.at[n], device_id=(plane, f), device_id_type=MESH
        )

    def sum_copies(k):
        ck, n = chunk(OUT, k), 6 * k
        return (
            remote(n, gs.at[half_of(opp, 0), :, ck], ta.at[:, :, ck], rs_send, rs_recv, up),
            remote(n + 1, gs.at[half_of(opp, 1), :, ck], tb.at[:, :, ck], rs_send, rs_recv, dn),
            remote(n + 2, gs.at[half_of(up, 1), :, ck], ra.at[high, :, ck], rs_send, rs_recv, up),
            remote(n + 3, gs.at[half_of(dn, 0), :, ck], rb.at[low, :, ck], rs_send, rs_recv, dn),
            remote(n + 4, ca.at[:, :, ck], ra.at[low, :, ck], rs_send, rs_recv, up),
            remote(n + 5, cb.at[:, :, ck], rb.at[high, :, ck], rs_send, rs_recv, dn),
        )

    sums = [sum_copies(k) for k in range(len(OUT))]

    def sum_pack(k):
        ck = chunk(OUT, k)

        def pack(e, _):
            gs[e, :, ck] = g[table[BLOCK_OF, e], :, ck]
            return 0

        lax.fori_loop(0, BLOCKS, pack, 0, unroll=8)

    def sum_first(k):
        for copy in sums[k][:4]:
            copy.start()

    def sum_far(k):
        sum_pack(k)
        for copy in sums[k][:2]:
            copy.start()

    def sum_near(k):
        for copy in sums[k][2:4]:
            copy.start()

    def sum_second(k):
        ck = chunk(OUT, k)

        def add_up(i, _):
            ca[i, :, ck] = bf16(f32(gs[up * SHARE + i, :, ck]) + f32(ta[i, :, ck]))
            return 0

        def add_dn(i, _):
            cb[i, :, ck] = bf16(f32(gs[dn * SHARE + HALF + i, :, ck]) + f32(tb[i, :, ck]))
            return 0

        sums[k][0].wait_recv()
        lax.fori_loop(0, HALF, add_up, 0, unroll=8)
        sums[k][4].start()
        sums[k][1].wait_recv()
        lax.fori_loop(0, HALF, add_dn, 0, unroll=8)
        sums[k][5].start()

    def offset(n):
        def step(i, size):
            return rem(size // 2 + div(i + 1, 2) * (1 - 2 * rem(i, 2)), size)

        return rem(z + step(div(n, NX), NZ), NZ) * NX + rem(x + step(rem(n, NX), NX), NX)

    def rows_of(rank):
        return pl.ds(pl.multiple_of(rank * ROWS, ROWS), ROWS)

    def forward(k):
        ck = chunk(OUT, k)
        for copy in sums[k][2:]:
            copy.wait_recv()

        def add(i, _):
            total = f32(gs[r * SHARE + i, :, ck]) + f32(ra[i, :, ck]) + f32(rb[i, :, ck])
            summed[i, :, ck] = bf16(total)
            return 0

        lax.fori_loop(0, SHARE, add, 0, unroll=8)

        def pack(q):
            outgoing[q, :, ck] = summed[table[CELL, r * COLUMNS + q], :, ck]

        def send(q):
            return pltpu.make_async_remote_copy(
                src_ref=outgoing.at[q, :, ck], dst_ref=s_ref.at[rows_of(f), ck], send_sem=f_send, recv_sem=f_recv.at[k],
                device_id=(r, 2 * q + worker), device_id_type=MESH,
            )

        def step(n, _):
            q = offset(n)
            pack(q)
            send(q).start()
            return 0

        lax.fori_loop(0, COLUMNS - 1, step, 0, unroll=True)
        pack(column)

        @pl.when(active)
        def _():
            pltpu.make_async_copy(outgoing.at[column, :, ck], s_ref.at[rows_of(f), ck], f_recv.at[k]).start()

        @pl.when(idle)
        def _():
            send(column).start()

    def products(first, count):
        part = chunk(OUT, first, count)
        for k in range(first, first + count):
            pltpu.make_async_copy(s_ref.at[:, chunk(OUT, k)], s_ref.at[:, chunk(OUT, k)], f_recv.at[k]).wait()
        pair = table[PAIR, r * COLUMNS + column]
        last = first + count == len(OUT)

        def step(t, carry):
            grad_sq, pre_sq = carry
            rows = pl.ds(pl.multiple_of(t * TILE, TILE), TILE)
            middle = bf16(jnp.dot(l_ref[pair, rows, :], s_ref[:, part], preferred_element_type=jnp.float32))
            pre = jnp.dot(middle, r_ref[pair, part, :], preferred_element_type=jnp.float32)
            if first > 0:
                pre = pre + pf[rows, :]
            pf[rows, :] = pre
            grad_sq = grad_sq + jnp.sum(jnp.square(f32(s_ref[rows, part])), axis=0, keepdims=True)
            if last:
                pre_sq = pre_sq + jnp.sum(jnp.square(pre), axis=0, keepdims=True)
            return grad_sq, pre_sq

        zeros = (jnp.zeros((1, part.size), jnp.float32), jnp.zeros((1, SIDE), jnp.float32))
        grad_sq, pre_sq = lax.fori_loop(0, SIDE // TILE, step, zeros)
        return jnp.sum(grad_sq, axis=1, keepdims=True), jnp.sum(pre_sq, axis=1, keepdims=True)

    def hand_over(k):
        rows = d_ref.at[:, 1 - worker, :, chunk(BACK, k)]
        return pltpu.make_async_remote_copy(
            src_ref=rows, dst_ref=rows, send_sem=d_send.at[k], recv_sem=d_recv.at[k], device_id=(r, sibling),
            device_id_type=MESH,
        )

    def backward(k):
        ck = chunk(BACK, k)

        @pl.when(active)
        def _():
            factor = factor_ref[...]

            def scale(t, _):
                part = pf[pl.ds(pl.multiple_of(t * 128, 128), 128), ck] * factor
                d_ref[pl.ds(t * 4, 4), :, :, ck] = bf16(part).reshape(4, 2, ROWS, BACK[k])
                return 0

            lax.fori_loop(0, SIDE // 128, scale, 0, unroll=8)
            hand_over(k).start()

        @pl.when(idle)
        def _():
            hand_over(k).wait_recv()

        def step(n, _):
            q = offset(n)
            pltpu.make_async_remote_copy(
                src_ref=d_ref.at[q, c, :, ck], dst_ref=back[k].at[column], send_sem=b_send, recv_sem=b_recv.at[k],
                device_id=(r, 2 * q + c), device_id_type=MESH,
            ).start()
            return 0

        lax.fori_loop(0, COLUMNS - 1, step, 0, unroll=True)
        pltpu.make_async_copy(d_ref.at[column, c, :, ck], back[k].at[column], b_recv.at[k]).start()

    def gather_copies(k):
        n = 6 * k

        def spread(m, plane, half, to):
            part = fin[k].at[half_of(plane, half)]
            return remote(n + m, part, part, ag_send, ag_recv, to)

        return (
            spread(0, r, 0, up), spread(1, r, 1, dn), spread(2, r, 1, up), spread(3, r, 0, dn), spread(4, dn, 0, up),
            spread(5, up, 1, dn),
        )

    gathers = [gather_copies(k) for k in range(len(BACK))]

    def gather_first(k):
        pltpu.make_async_copy(back[k], back[k], b_recv.at[k]).wait()

        def place(i, _):
            e = r * SHARE + i
            fin[k][e] = back[k][table[COLUMN_OF, e]]
            return 0

        lax.fori_loop(0, SHARE, place, 0, unroll=8)
        for copy in gathers[k][:4]:
            copy.start()

    def gather_second(k):
        gathers[k][0].wait_recv()
        gathers[k][4].start()
        gathers[k][1].wait_recv()
        gathers[k][5].start()

    def finish(k):
        ck = chunk(BACK, k)
        for copy in gathers[k][2:]:
            copy.wait_recv()

        def place(b, _):
            o[b, :, ck] = fin[k][table[ENTRY_OF, b]]
            return 0

        lax.fori_loop(0, BLOCKS, place, 0, unroll=8)

    load_g.wait()
    load_table.wait()
    sum_pack(0)
    pl.semaphore_wait(barrier, 17)
    sum_first(0)

    def greet_plane(d, _):
        pl.semaphore_signal(plane_sem, inc=1, device_id=z_peer(d), device_id_type=MESH)
        return 0

    lax.fori_loop(1, 8, greet_plane, 0)

    @pl.when(active)
    def _():
        load_l.start()
        load_r.start()

    @pl.when(idle)
    def _():
        give_l.start()
        give_r.start()

    sum_pack(1)
    sum_second(0)
    sum_first(1)
    pl.semaphore_wait(plane_sem, 7)
    forward(0)
    sum_second(1)
    sum_pack(2)
    sum_first(2)
    forward(1)
    sum_second(2)
    sum_pack(3)
    sum_first(3)
    forward(2)
    sum_second(3)
    forward(3)

    @pl.when(active)
    def _():
        load_l.wait()
        load_r.wait()
        give_l.wait_recv()
        give_r.wait_recv()
        grad_ms, pre_sq = jnp.zeros((1, 1), jnp.float32), None
        for first, count in PARTS:
            grad_sq, pre_sq = products(first, count)
            grad_ms = grad_ms + grad_sq / (SIDE * SIDE)
        pre_ms = pre_sq / (SIDE * SIDE)
        factor_ref[...] = jnp.sqrt(grad_ms) * lax.rsqrt(pre_ms + EPSILON)

    for k in range(len(BACK) + 3):
        if k < len(BACK):
            backward(k)
        if 1 <= k <= len(BACK):
            gather_first(k - 1)
        if 2 <= k <= len(BACK) + 1:
            gather_second(k - 2)
        if k >= 3:
            finish(k - 3)

    for copies in sums + gathers:
        for copy in copies:
            copy.wait_send()

    sent = d_ref.at[pl.ds(1, COLUMNS - 1), 0]
    pltpu.make_async_copy(sent, sent, b_send).wait()

    @pl.when(active)
    def _():
        sent = outgoing.at[pl.ds(1, COLUMNS - 1)]
        pltpu.make_async_copy(sent, sent, f_send).wait()
        for k in range(len(BACK)):
            hand_over(k).wait_send()

    @pl.when(idle)
    def _():
        pltpu.make_async_copy(outgoing, outgoing, f_send).wait()
        give_l.wait_send()
        give_r.wait_send()


def on_device(grads, block_owner, left_roots, right_roots):
    anywhere = pl.BlockSpec(memory_space=pltpu.HBM)
    share = pltpu.VMEM((SHARE, ROWS, SIDE), jnp.bfloat16)
    half = pltpu.VMEM((HALF, ROWS, SIDE), jnp.bfloat16)
    column = pltpu.VMEM((COLUMNS, ROWS, SIDE), jnp.bfloat16)
    whole = pltpu.VMEM((BLOCKS, ROWS, SIDE), jnp.bfloat16)
    square = pltpu.VMEM((SIDE, SIDE), jnp.bfloat16)
    roots = pltpu.VMEM((4, SIDE, SIDE), jnp.bfloat16)
    dma = pltpu.SemaphoreType.DMA
    return pl.pallas_call(
        kernel,
        out_shape=jax.ShapeDtypeStruct((BLOCKS, ROWS, SIDE), jnp.bfloat16),
        in_specs=[pl.BlockSpec(memory_space=pltpu.SMEM), anywhere, anywhere, anywhere],
        out_specs=pl.BlockSpec(memory_space=pltpu.VMEM),
        scratch_shapes=[
            pltpu.VMEM((BLOCKS, 128), jnp.int32), pltpu.VMEM((8, 128), jnp.int32), pltpu.SMEM((8, 128), jnp.int32),
            whole, whole, half, half, half, half, share, share, share, column, square, roots, roots,
            pltpu.VMEM((SIDE, SIDE), jnp.float32), pltpu.VMEM((1, 1), jnp.float32), pltpu.VMEM((COLUMNS, 2, ROWS, SIDE), jnp.bfloat16),
            dma((4,)), dma((2,)), dma((2,)), dma((6 * len(OUT),)), dma((6 * len(OUT),)), dma, dma((len(OUT),)), dma, dma((len(BACK),)),
            dma((len(BACK),)), dma((len(BACK),)), dma((6 * len(BACK),)), dma((6 * len(BACK),)), pltpu.SemaphoreType.REGULAR,
            *[pltpu.VMEM((COLUMNS, ROWS, width), jnp.bfloat16) for width in BACK],
            *[pltpu.VMEM((BLOCKS, ROWS, width), jnp.bfloat16) for width in BACK],
        ],
        compiler_params=pltpu.CompilerParams(
            collective_id=0, has_side_effects=True, vmem_limit_bytes=51 * 1024 * 1024
        ),
        cost_estimate=pl.CostEstimate(flops=4 * SIDE**3, bytes_accessed=12 * 1024 * 1024, transcendentals=0),
    )(block_owner, grads, left_roots, right_roots)


def solution(mesh):
    in_specs = (P("replica", None, "fsdp", None), P(), P("fsdp", None, None), P("fsdp", None, None))
    return jax.shard_map(
        on_device, mesh=mesh, in_specs=in_specs, out_specs=P(None, "fsdp", None), check_vma=False
    )
```
